256 devices in a mesh: dp: 16 (over z, core), section: 16 (over x, y).
Axes of the slice: x: 4, y: 4, z: 8, core: 2. Of those that a mesh axis runs over, the one named last changes fastest.
Arguments:
- layer_inputs: bfloat16 [16, 16, 512, 2048], P('section', 'dp'), may hold values from -24 to 24
- output_grads: bfloat16 [16, 16, 512, 4608], P('section', 'dp'), may hold values from -5.0351435e-05 to 5.0351435e-05
- lengths: int32 [16], P('dp'), may hold values from 1 to 512, as said below
Outputs:
- clipped_grad: bfloat16 [16, 2048, 4608], P('section', 'dp')
The draws below stay inside these ranges and needn't reach their ends.
Inputs may be any that keep to these rules, and one draw needn't show every extreme that they name: `lengths`: some example has all 512 tokens live.
All inputs are finite; a program needn't handle non-finite values.
Results may differ from the reference program's by a relative error of at most 0.024.
Values may be sent and summed in bfloat16 or wider, within the bound.
A program may use at most 128 MiB of HBM per device.

```python
import math
import jax
import jax.numpy as jnp
from jax import lax

DIN = 2048
DOUT = 4608
SEQ = 512
EX_DEV = 1
EXAMPLES = 16
LAYERS = 16
N_DP = 16


def token_rows(key, width, share):
    first, second = jax.random.split(key)
    common = jax.random.truncated_normal(first, -4.0, 4.0, (LAYERS, EXAMPLES, 1, width), jnp.float32)
    single = jax.random.truncated_normal(second, -4.0, 4.0, (LAYERS, EXAMPLES, SEQ, width), jnp.float32)
    return math.sqrt(share) * common + math.sqrt(1.0 - share) * single


def layer_ramp(base):
    steps = jnp.arange(LAYERS, dtype=jnp.float32) / float(max(LAYERS - 1, 1))
    ramp = base ** steps
    return ramp / jnp.sqrt(jnp.mean(ramp * ramp))


def draw_layer_inputs(key, part):
    key = jax.random.fold_in(key, 11)
    first, second = jax.random.split(key)
    share = 0.05
    values = token_rows(first, DIN, share)
    groups = EXAMPLES // EX_DEV
    order = jax.random.permutation(second, groups)
    owner = order[jnp.arange(EXAMPLES) // EX_DEV]
    column_block = jnp.arange(DIN) // (DIN // groups)
    boost = jnp.where(column_block[None, :] == owner[:, None], 4.0, 1.0).astype(jnp.float32)
    return (values * boost[None, :, None, :]).astype(jnp.bfloat16)


def draw_output_grads(key, part):
    key = jax.random.fold_in(key, 23)
    share = 0.05
    base = 2.0
    scale = 2.0 * (SEQ * (1.0 + SEQ / 400.0) * DIN * DOUT * LAYERS) ** (-0.5)
    values = token_rows(key, DOUT, share)
    ramp = layer_ramp(base)
    return (scale * ramp[:, None, None, None] * values).astype(jnp.bfloat16)


def draw_lengths(key, part):
    key = jax.random.fold_in(key, 7)
    first, second = jax.random.split(key)
    drawn = jax.random.randint(first, (EXAMPLES,), 1, SEQ + 1)
    where_full = jax.random.randint(second, (), 0, EXAMPLES)
    return jnp.where(jnp.arange(EXAMPLES) == where_full, SEQ, drawn).astype(jnp.int32)


def setup_inputs(seed: int = 0) -> dict:
    arg_keys = jax.random.split(jax.random.key(seed), 4)
    layer_inputs = draw_layer_inputs(jax.random.fold_in(arg_keys[3], 71), 0)
    output_grads = draw_output_grads(jax.random.fold_in(arg_keys[3], 71), 0)
    lengths = draw_lengths(jax.random.fold_in(arg_keys[3], 71), 0)
    return {"layer_inputs": layer_inputs, "output_grads": output_grads, "lengths": lengths}


def ghost_norm(pair):
    inputs, grads = pair
    gram_in = jnp.dot(inputs, inputs.T, preferred_element_type=jnp.float32)
    gram_out = jnp.dot(grads, grads.T, preferred_element_type=jnp.float32)
    return jnp.sum(gram_in * gram_out)

def reference(layer_inputs, output_grads, lengths):
    positions = jnp.arange(SEQ, dtype=jnp.int32)
    live = positions[None, :] < lengths[:, None]
    masked = jnp.where(live[None, :, :, None], output_grads, jnp.zeros_like(output_grads))

    def layer_norms(pair):
        return lax.map(ghost_norm, pair)
    norms = lax.map(layer_norms, (layer_inputs, masked))
    total = lax.optimization_barrier(jnp.sum(norms, axis=0))
    factor = jnp.minimum(1.0, 1.0 / jnp.sqrt(total + 1e-06))
    scaled = (factor[None, :, None, None] * masked.astype(jnp.float32)).astype(jnp.bfloat16)
    weight = math.sqrt(DIN * DOUT * LAYERS / EXAMPLES)

    def layer_grad(pair):
        inputs, grads = pair
        inputs = inputs.reshape(N_DP, EX_DEV * SEQ, DIN)
        grads = grads.reshape(N_DP, EX_DEV * SEQ, DOUT)

        def add_group(carry, group):
            term = lax.dot_general(group[0], group[1], (((0,), (0,)), ((), ())), preferred_element_type=jnp.float32)
            rounded = lax.optimization_barrier(term.astype(jnp.bfloat16))
            return (carry + rounded.astype(jnp.float32), None)
        summed, _ = lax.scan(add_group, jnp.zeros((DIN, DOUT), jnp.float32), (inputs, grads))
        return (summed * weight).astype(jnp.bfloat16)
    return lax.map(layer_grad, (layer_inputs, scaled))
```

```python
import functools
import math

import jax
import jax.numpy as jnp
from jax import lax
from jax.experimental import pallas as pl
from jax.experimental.pallas import tpu as pltpu
from jax.sharding import PartitionSpec as P

F32 = jnp.float32
BF16 = jnp.bfloat16
MESH = pl.DeviceIdType.MESH
PIECES = 3


def kernel(dims, weight, len_ref, x_ref, g_ref, out_ref, xv, xb, gv, xt, sendb, recvb, fin, gin, gout, tile, norms, lens,
           facs, xe, sendu, recvu, upfac, pre, xe_sem, early_send, early_recv, up_send, up_recv, xv_sem, xb_sem, gv_sem, xb_send, gv_send, len_sem, norm_send, norm_recv, fac_sem, ring_send, ring_recv):
    n_chips, n_sec, rows = dims
    seq = x_ref.shape[0]
    width = gv.shape[2]
    chunks = 2 * PIECES
    half = seq // 2
    steps = n_chips - 1
    dp = lax.axis_index("dp")
    sec = lax.axis_index("section")
    z = lax.div(dp, 2)
    core = lax.rem(dp, 2)
    partner = dp + 1 - 2 * core
    ahead = lax.rem(dp + 2, 2 * n_chips)
    behind = lax.rem(dp + 2 * n_chips - 2, 2 * n_chips)
    ring_to = (ahead, behind)

    xe_cols = pl.ds(pl.multiple_of(lax.rem(z + n_chips // 2, n_chips) * 2 * rows, 128), 2 * rows)
    xe_copy = pltpu.make_async_copy(x_ref.at[:, xe_cols], xe, xe_sem)
    xe_copy.start()
    x_copy = pltpu.make_async_copy(x_ref, xv, xv_sem)

    def g_copy(c):
        cols = pl.ds(pl.multiple_of(c * width, 128), width)
        return pltpu.make_async_copy(g_ref.at[:, cols], gv.at[c, pl.ds(0, seq)], gv_sem.at[0, c])

    def g_swap(c):
        cols = pl.ds(pl.multiple_of(c * width, 128), width)
        return pltpu.make_async_remote_copy(
            g_ref.at[:, cols], gv.at[c, pl.ds(seq, seq)], gv_send.at[c], gv_sem.at[1, c],
            device_id=(partner, sec), device_id_type=MESH)

    def owner(k):
        far = lax.div(k + 1, 2)
        turn = jnp.where(lax.rem(k, 2) == 1, n_chips - far, far)
        return lax.rem(z + n_chips // 2 + turn, n_chips)

    def x_cols(k, c):
        return pl.ds(pl.multiple_of((2 * k + c) * rows, 128), rows)

    def xb_copy(k):
        return pltpu.make_async_copy(x_ref.at[:, x_cols(k, core)], xb.at[0, k], xb_sem.at[0, k])

    def xb_swap(k):
        return pltpu.make_async_remote_copy(
            x_ref.at[:, x_cols(k, 1 - core)], xb.at[1, k], xb_send.at[k], xb_sem.at[1, k],
            device_id=(partner, sec), device_id_type=MESH)

    for d in range(2):
        g_copy(d * PIECES).start()
    x_copy.start()

    barrier = pltpu.get_barrier_semaphore()
    for peer in (partner, ahead, behind, ahead + partner - dp, behind + partner - dp):
        pl.semaphore_signal(barrier, inc=1, device_id=(peer, sec), device_id_type=MESH)

    @pl.loop(1, n_sec)
    def _(j):
        pl.semaphore_signal(barrier, inc=1, device_id=(dp, lax.rem(sec + j, n_sec)), device_id_type=MESH)

    @pl.loop(1, PIECES)
    def _(s):
        for d in range(2):
            g_copy(d * PIECES + s).start()

    @pl.loop(0, n_chips)
    def _(k):
        xb_copy(owner(k)).start()

    lens[0] = jnp.full(lens.shape[1:], len_ref[0], F32)

    xe_copy.wait()
    token = lax.broadcasted_iota(jnp.int32, xe.shape, 0)
    xet = jnp.where(token < len_ref[0], xe[...].astype(F32), 0.0).T.astype(BF16)
    for d in range(2):
        g_copy(d * PIECES).wait()
        early = jnp.dot(xet, gv[d * PIECES, :seq], preferred_element_type=F32).astype(BF16)
        for e in range(2):
            sendu[d, e] = early[e * rows:(e + 1) * rows]

    def early_copy(d, e):
        slot = lax.rem(core + e, 2)
        return pltpu.make_async_remote_copy(
            sendu.at[d, e], recvu.at[d, slot], early_send.at[d, e], early_recv.at[d, slot],
            device_id=(ring_to[d] - core + e, sec), device_id_type=MESH)

    def early_wait(d, slot):
        pltpu.make_async_remote_copy(
            sendu.at[d, slot], recvu.at[d, slot], early_send.at[d, slot], early_recv.at[d, slot],
            device_id=(ring_to[d], sec), device_id_type=MESH).wait_recv()

    pl.semaphore_wait(barrier, n_sec + 4)
    for e in range(2):
        for d in range(2):
            early_copy(d, e).start()

    len_swap = pltpu.make_async_remote_copy(
        lens.at[0], lens.at[1], len_sem.at[0], len_sem.at[1], device_id=(partner, sec), device_id_type=MESH)
    len_swap.start()

    xb_swap(owner(0)).start()
    for d in range(2):
        g_swap(d * PIECES + 1).start()

    def gram(acc, block, first):
        nt = (((1,), (1,)), ((), ()))
        left = lax.dot_general(block[:half], block[:half], nt, preferred_element_type=F32)
        right = lax.dot_general(block, block[half:], nt, preferred_element_type=F32)
        if first:
            acc[:half, :half] = left
            acc[:, half:] = right
        else:
            acc[:half, :half] += left
            acc[:, half:] += right

    x_copy.wait()
    span = 1024
    for j in range(xv.shape[1] // span):
        gram(gin, xv[:, j * span:(j + 1) * span], j == 0)

    @pl.loop(1, 3)
    def _(k):
        xb_swap(owner(k)).start()

    for s in list(range(2, PIECES)) + [0]:
        for d in range(2):
            g_swap(d * PIECES + s).start()

    @pl.loop(3, n_chips)
    def _(k):
        xb_swap(owner(k)).start()

    gram(gout, gv[0, :seq], True)
    gram(gout, gv[PIECES, :seq], False)

    @pl.loop(1, PIECES)
    def _(s):
        for d in range(2):
            c = d * PIECES + s
            g_copy(c).wait()
            gram(gout, gv[c, :seq], False)

    row = lax.broadcasted_iota(jnp.int32, (seq, half), 0)
    col = lax.broadcasted_iota(jnp.int32, (seq, half), 1)
    n_live = len_ref[0]
    left_live = (row[:half] < n_live) & (col[:half] < n_live)
    left = jnp.where(left_live, gin[:half, :half] * gout[:half, :half], 0.0)
    twice = jnp.where(row < half, 2.0, 1.0)
    right_live = (row < n_live) & (col + half < n_live)
    right = jnp.where(right_live, gin[:, half:] * gout[:, half:] * twice, 0.0)
    cells = left + right[:half] + right[half:]
    norm = jnp.sum(jnp.sum(cells, axis=0, keepdims=True), axis=1, keepdims=True)
    tile[...] = jnp.broadcast_to(norm, tile.shape)
    norms[sec] = tile[...]

    def norm_copy(j, frm, to):
        return pltpu.make_async_remote_copy(
            tile, norms.at[frm], norm_send.at[j], norm_recv.at[frm], device_id=(dp, to), device_id_type=MESH)

    @pl.loop(1, n_sec)
    def _(j):
        norm_copy(j, sec, lax.rem(sec + j, n_sec)).start()

    len_swap.wait_recv()
    token = lax.broadcasted_iota(jnp.int32, (seq, rows), 0).astype(F32)

    def turn(k):
        xb_copy(k).wait()
        xb_swap(k).wait_recv()
        for e in range(2):
            block = jnp.where(token < lens[e, 0:1, :], xb[e, k].astype(F32), 0.0)
            xt[k, :, e * seq:(e + 1) * seq] = block.T.astype(BF16)

    def scale(k):
        for e in range(2):
            factor = facs[e, 0:1, :]
            for j in range(seq // 128):
                cols = slice(e * seq + j * 128, e * seq + (j + 1) * 128)
                xt[k, :, cols] = (xt[k, :, cols].astype(F32) * factor).astype(BF16)

    turn(owner(0))
    for d in range(2):
        c = d * PIECES + 1
        g_swap(c).wait_recv()
        for e in range(2):
            tokens = slice(e * seq, (e + 1) * seq)
            pre[d, e] = jnp.dot(xt[owner(0), :, tokens], gv[c, tokens], preferred_element_type=F32)

    @pl.loop(1, 3)
    def _(k):
        turn(owner(k))

    @pl.loop(1, n_sec)
    def _(j):
        frm = lax.rem(sec + j, n_sec)
        norm_copy(j, frm, frm).wait_recv()

    total = jnp.sum(norms[...], axis=0)
    facs[0] = jnp.minimum(1.0, 1.0 / jnp.sqrt(total + 1e-06))
    fac_swap = pltpu.make_async_remote_copy(
        facs.at[0], facs.at[1], fac_sem.at[0], fac_sem.at[1], device_id=(partner, sec), device_id_type=MESH)
    fac_swap.start()
    fac_swap.wait_recv()

    def up_copy(d):
        return pltpu.make_async_remote_copy(
            facs, upfac.at[d], up_send.at[d], up_recv.at[d], device_id=(ring_to[d], sec), device_id_type=MESH)

    def ring_copy(d, i, s):
        return pltpu.make_async_remote_copy(
            sendb.at[d, i, s], recvb.at[d, i, s], ring_send.at[d, i, s], ring_recv.at[d, i, s],
            device_id=(ring_to[d], sec), device_id_type=MESH)

    def term(k, c):
        return jnp.dot(xt[k], gv[c], preferred_element_type=F32)

    def target(d, i):
        dist = n_chips // 2 - lax.div(i + 1, 2)
        return lax.rem(z + dist, n_chips) if d == 0 else lax.rem(z + n_chips - dist, n_chips)

    def chunk(d, i, s):
        return lax.rem(i + d, 2) * PIECES + s

    def place(n):
        return lax.div(n, PIECES), lax.rem(n, PIECES)

    def pieces(first, last, paced=True):
        @pl.loop(first, last)
        def _(n):
            i, s = place(n)
            for d in range(2):
                c = chunk(d, i, s)
                if last <= PIECES:
                    g_swap(c).wait_recv()
                part = term(target(d, i), c)
                if first == 2 * PIECES:
                    up_copy(d).wait_recv()
                    for e in range(2):
                        early_wait(d, e)
                        part += recvu[d, e].astype(F32) * across(upfac[d, e, 0:1])
                elif first > 2 * PIECES:
                    ring_copy(d, i - 2, s).wait_recv()
                    part += recvb[d, i - 2, s].astype(F32)
                sendb[d, i, s] = part.astype(BF16)
                if paced:
                    ring_copy(d, *place(n - 2)).wait_send()
                ring_copy(d, i, s).start()

    def across(factor):
        return jnp.concatenate([factor] * (width // 128), axis=1)

    for d in range(2):
        sendb[d, 0, 1] = (pre[d, 0] * across(facs[0, 0:1]) + pre[d, 1] * across(facs[1, 0:1])).astype(BF16)
        ring_copy(d, 0, 1).start()
    for d in range(2):
        up_copy(d).start()
    scale(owner(0))
    pieces(2, PIECES, paced=False)

    @pl.loop(1, 3)
    def _(k):
        scale(owner(k))

    for d in range(2):
        g_swap(d * PIECES).wait_recv()
    pieces(PIECES, 2 * PIECES)

    @pl.loop(3, n_chips)
    def _(k):
        turn(owner(k))
        scale(owner(k))

    pieces(2 * PIECES, 2 * PIECES + 1)
    pieces(2 * PIECES + 1, steps * PIECES)

    @pl.loop(0, PIECES)
    def _(s):
        for d in range(2):
            c = d * PIECES + s
            part = term(z, c)
            ring_copy(1 - d, steps - 2, s).wait_recv()
            fin[c] = part + recvb[1 - d, steps - 2, s].astype(F32)

    for s in range(PIECES):
        for d in range(2):
            c = d * PIECES + s
            ring_copy(d, steps - 1, s).wait_recv()
            done = (fin[c] + recvb[d, steps - 1, s].astype(F32)) * weight
            out_ref[:, c * width:(c + 1) * width] = done.astype(out_ref.dtype)

    len_swap.wait_send()
    fac_swap.wait_send()
    for d in range(2):
        up_copy(d).wait_send()
        for e in range(2):
            early_copy(d, e).wait_send()

    @pl.loop(1, n_sec)
    def _(j):
        norm_copy(j, sec, lax.rem(sec + j, n_sec)).wait_send()

    @pl.loop(0, chunks)
    def _(c):
        g_swap(c).wait_send()

    @pl.loop(0, n_chips)
    def _(k):
        xb_swap(k).wait_send()

    for d in range(2):
        for s in (PIECES - 2, PIECES - 1):
            ring_copy(d, steps - 1, s).wait_send()


def shards(layer_inputs, output_grads, lengths):
    n_dp, n_sec = lax.axis_size("dp"), lax.axis_size("section")
    inputs = layer_inputs[0, 0]
    grads = output_grads[0, 0]
    seq, din = inputs.shape
    dout = grads.shape[1]
    rows = din // n_dp
    n_chips = n_dp // 2
    chunks = 2 * PIECES
    width = dout // chunks
    weight = math.sqrt(din * dout * n_sec / n_dp)
    dma = pltpu.SemaphoreType.DMA
    ring = (2, n_chips - 1, PIECES)
    out = pl.pallas_call(
        functools.partial(kernel, (n_chips, n_sec, rows), weight),
        out_shape=jax.ShapeDtypeStruct((rows, dout), BF16),
        in_specs=[
            pl.BlockSpec(memory_space=pltpu.SMEM),
            pl.BlockSpec(memory_space=pl.ANY),
            pl.BlockSpec(memory_space=pl.ANY),
        ],
        out_specs=pl.BlockSpec(memory_space=pltpu.VMEM),
        scratch_shapes=[
            pltpu.VMEM((seq, din), BF16),
            pltpu.VMEM((2, n_chips, seq, rows), BF16),
            pltpu.VMEM((chunks, 2 * seq, width), BF16),
            pltpu.VMEM((n_chips, rows, 2 * seq), BF16),
            pltpu.VMEM(ring + (rows, width), BF16),
            pltpu.VMEM(ring + (rows, width), BF16),
            pltpu.VMEM((chunks, rows, width), F32),
            pltpu.VMEM((seq, seq), F32),
            pltpu.VMEM((seq, seq), F32),
            pltpu.VMEM((8, 128), F32),
            pltpu.VMEM((n_sec, 8, 128), F32),
            pltpu.VMEM((2, 8, 128), F32),
            pltpu.VMEM((2, 8, 128), F32),
            pltpu.VMEM((seq, 2 * rows), BF16),
            pltpu.VMEM((2, 2, rows, width), BF16),
            pltpu.VMEM((2, 2, rows, width), BF16),
            pltpu.VMEM((2, 2, 8, 128), F32),
            pltpu.VMEM((2, 2, rows, width), F32),
            dma,
            dma((2, 2)),
            dma((2, 2)),
            dma((2,)),
            dma((2,)),
            dma,
            dma((2, n_chips)),
            dma((2, chunks)),
            dma((n_chips,)),
            dma((chunks,)),
            dma((2,)),
            dma((n_sec,)),
            dma((n_sec,)),
            dma((2,)),
            dma(ring),
            dma(ring),
        ],
        compiler_params=pltpu.CompilerParams(
            collective_id=0, has_side_effects=True, vmem_limit_bytes=52 * 2**20
        ),
        cost_estimate=pl.CostEstimate(
            flops=2 * seq * din * dout + 2 * seq * seq * (din + dout), bytes_accessed=2 * seq * (din + dout),
            transcendentals=0,
        ),
    )(lengths, inputs, grads)
    return out[None]


def solution(mesh):
    placed = (P("section", "dp", None, None), P("section", "dp", None, None), P("dp"))
    return jax.shard_map(
        shards, mesh=mesh, in_specs=placed, out_specs=P("section", "dp", None), check_vma=False
    )
```

```python
import functools
import math

import jax
import jax.numpy as jnp
from jax import lax
from jax.experimental import pallas as pl
from jax.experimental.pallas import tpu as pltpu
from jax.sharding import PartitionSpec as P

F32 = jnp.float32
BF16 = jnp.bfloat16
MESH = pl.DeviceIdType.MESH
PIECES = 3
EARLY = 2


def kernel(dims, weight, len_ref, x_ref, g_ref, out_ref, xe, xv, xb, gv, xt, sendb, recvb, sendu, recvu, pre, fin, gin, gout,
           row_tile, col_tile, rows_in, cols_in, lens, facs, upfac, xe_sem, xv_sem, g_sem, xb_send, xb_recv, g_send, g_recv,
           len_sem, row_send, row_recv, col_send, col_recv, early_send, early_recv, up_send, up_recv, ring_send, ring_recv):
    n_chips, side, rows = dims
    seq = x_ref.shape[0]
    half = sendb.shape[3]
    width = half // PIECES
    gone = EARLY * width
    mid = seq // 2
    steps = n_chips - 1
    dp = lax.axis_index("dp")
    sec = lax.axis_index("section")
    z = lax.div(dp, 2)
    core = lax.rem(dp, 2)
    partner = dp + 1 - 2 * core
    ahead = lax.rem(dp + 2, 2 * n_chips)
    behind = lax.rem(dp + 2 * n_chips - 2, 2 * n_chips)
    ring_to = (ahead, behind)
    sec_x = lax.div(sec, side)
    sec_y = lax.rem(sec, side)

    def in_row(j):
        return lax.rem(sec_x + j, side) * side + sec_y

    def in_col(j):
        return sec_x * side + lax.rem(sec_y + j, side)

    def owner(k):
        far = lax.div(k + 1, 2)
        turn = jnp.where(lax.rem(k, 2) == 1, n_chips - far, far)
        return lax.rem(z + n_chips // 2 + turn, n_chips)

    def x_cols(k, c):
        return pl.ds(pl.multiple_of((2 * k + c) * rows, 128), rows)

    def g_cols(h, part):
        return pl.ds(h * half + gone, half - gone) if part else pl.ds(h * half, gone)

    def g_copy(h, part):
        cols = g_cols(h, part)
        return pltpu.make_async_copy(g_ref.at[:, cols], gv.at[pl.ds(0, seq), cols], g_sem.at[h, part])

    def g_swap(h, part):
        cols = g_cols(h, part)
        return pltpu.make_async_remote_copy(
            g_ref.at[:, cols], gv.at[pl.ds(seq, seq), cols], g_send.at[h, part], g_recv.at[h, part],
            device_id=(partner, sec), device_id_type=MESH)

    def xb_swap(k):
        return pltpu.make_async_remote_copy(
            x_ref.at[:, x_cols(k, 1 - core)], xb.at[k], xb_send.at[k], xb_recv.at[k],
            device_id=(partner, sec), device_id_type=MESH)

    first = owner(0)
    xe_cols = pl.ds(pl.multiple_of(2 * first * rows, 128), 2 * rows)
    xe_copy = pltpu.make_async_copy(x_ref.at[:, xe_cols], xe, xe_sem)
    x_copy = pltpu.make_async_copy(x_ref, xv, xv_sem)
    xe_copy.start()
    for h in range(2):
        g_copy(h, 0).start()
    x_copy.start()
    for h in range(2):
        g_copy(h, 1).start()

    barrier = pltpu.get_barrier_semaphore()
    peers = [(peer + other, sec) for peer in ring_to for other in (0, partner - dp)]
    peers += [(dp, in_row(j)) for j in range(1, side)] + [(dp, in_col(j)) for j in range(1, side)]
    peers += [(partner, in_col(j)) for j in range(side)]
    for peer in peers:
        pl.semaphore_signal(barrier, inc=1, device_id=peer, device_id_type=MESH)

    xe_copy.wait()
    token = lax.broadcasted_iota(jnp.int32, xe.shape, 0)
    xet = jnp.where(token < len_ref[0], xe[...].astype(F32), 0.0).T.astype(BF16)

    def early_copy(d, p, e):
        slot = lax.rem(core + e, 2)
        return pltpu.make_async_remote_copy(
            sendu.at[d, p, e], recvu.at[d, p, slot], early_send.at[d, p, e], early_recv.at[d, p, slot],
            device_id=(ring_to[d] - core + e, sec), device_id_type=MESH)

    def early_wait(d, p, slot):
        pltpu.make_async_remote_copy(
            sendu.at[d, p, slot], recvu.at[d, p, slot], early_send.at[d, p, slot], early_recv.at[d, p, slot],
            device_id=(ring_to[d], sec), device_id_type=MESH).wait_recv()

    def early_terms(p):
        for d in range(2):
            if p == 0:
                g_copy(d, 0).wait()
            lo = d * half + p * width
            early = jnp.dot(xet, gv[:seq, lo:lo + width], preferred_element_type=F32).astype(BF16)
            for e in range(2):
                sendu[d, p, e] = early[e * rows:(e + 1) * rows]

    def early_start(p):
        for e in range(2):
            for d in range(2):
                early_copy(d, p, e).start()

    early_terms(0)
    lens[0] = jnp.full(lens.shape[1:], len_ref[0], F32)
    pl.semaphore_wait(barrier, len(peers))
    early_start(0)
    len_swap = pltpu.make_async_remote_copy(
        lens.at[0], lens.at[1], len_sem.at[0], len_sem.at[1], device_id=(partner, sec), device_id_type=MESH)
    len_swap.start()
    xb_swap(first).start()
    for h in range(2):
        g_swap(h, 1).start()

    def gram(acc, block, new=False):
        nt = (((1,), (1,)), ((), ()))
        left = lax.dot_general(block[:mid], block[:mid], nt, preferred_element_type=F32)
        right = lax.dot_general(block, block[mid:], nt, preferred_element_type=F32)
        if new:
            acc[:mid, :mid] = left
            acc[:, mid:] = right
        else:
            acc[:mid, :mid] += left
            acc[:, mid:] += right

    x_copy.wait()
    span = 1024
    for j in range(0, xv.shape[1], span):
        gram(gin, xv[:, j:j + span], j == 0)
    for p in range(1, EARLY):
        early_terms(p)
        early_start(p)
    for h in range(2):
        for j in range(0, gone, width):
            gram(gout, gv[:seq, h * half + j:h * half + j + width], h == 0 and j == 0)
    for h in range(2):
        g_copy(h, 1).wait()
        for j in range(gone, half, span):
            gram(gout, gv[:seq, h * half + j:h * half + min(j + span, half)])

    row = lax.broadcasted_iota(jnp.int32, (seq, mid), 0)
    col = lax.broadcasted_iota(jnp.int32, (seq, mid), 1)
    n_live = len_ref[0]
    left_live = (row[:mid] < n_live) & (col[:mid] < n_live)
    left = jnp.where(left_live, gin[:mid, :mid] * gout[:mid, :mid], 0.0)
    twice = jnp.where(row < mid, 2.0, 1.0)
    right_live = (row < n_live) & (col + mid < n_live)
    right = jnp.where(right_live, gin[:, mid:] * gout[:, mid:] * twice, 0.0)
    cells = left + right[:mid] + right[mid:]
    norm = jnp.sum(jnp.sum(cells, axis=0, keepdims=True), axis=1, keepdims=True)
    row_tile[...] = jnp.broadcast_to(norm, row_tile.shape)

    def row_copy(j, frm):
        return pltpu.make_async_remote_copy(
            row_tile, rows_in.at[frm], row_send.at[j], row_recv.at[frm], device_id=(dp, in_row(j)), device_id_type=MESH)

    def col_copy(e, j, frm):
        return pltpu.make_async_remote_copy(
            col_tile, cols_in.at[e, frm], col_send.at[e, j], col_recv.at[e, frm],
            device_id=(partner if e else dp, in_col(j)), device_id_type=MESH)

    for j in range(1, side):
        row_copy(j, sec_x).start()
    rows_in[sec_x] = row_tile[...]

    token = lax.broadcasted_iota(jnp.int32, (seq, rows), 0).astype(F32)

    def turn(k):
        xb_swap(k).wait_recv()
        for e, block in enumerate((xv[:, x_cols(k, core)], xb[k])):
            block = jnp.where(token < lens[e, 0:1, :], block.astype(F32), 0.0)
            xt[k, :, e * seq:(e + 1) * seq] = block.T.astype(BF16)

    def scale(k):
        for e in range(2):
            factor = facs[e, 0:1, :]
            for j in range(seq // 128):
                cols = slice(e * seq + j * 128, e * seq + (j + 1) * 128)
                xt[k, :, cols] = (xt[k, :, cols].astype(F32) * factor).astype(BF16)

    len_swap.wait_recv()
    turn(first)

    for j in range(1, side):
        row_copy(j, lax.rem(sec_x + j, side)).wait_recv()
    col_tile[...] = jnp.sum(rows_in[...], axis=0)
    for j in range(side):
        col_copy(1, j, sec_y).start()
        if j:
            col_copy(0, j, sec_y).start()
    cols_in[0, sec_y] = col_tile[...]

    rest = [(s * width, (s + 1) * width) for s in range(EARLY, PIECES)]
    for d in range(2):
        g_swap(d, 1).wait_recv()
        for lo, hi in rest:
            for e in range(2):
                tokens = slice(e * seq, (e + 1) * seq)
                pre[d, e, :, lo - gone:hi - gone] = jnp.dot(
                    xt[first, :, tokens], gv[tokens, d * half + lo:d * half + hi], preferred_element_type=F32)

    for j in range(side):
        frm = lax.rem(sec_y + j, side)
        col_copy(1, j, frm).wait_recv()
        if j:
            col_copy(0, j, frm).wait_recv()
    for e in range(2):
        facs[e] = jnp.minimum(1.0, 1.0 / jnp.sqrt(jnp.sum(cols_in[e], axis=0) + 1e-06))

    def up_copy(d):
        return pltpu.make_async_remote_copy(
            facs, upfac.at[d], up_send.at[d], up_recv.at[d], device_id=(ring_to[d], sec), device_id_type=MESH)

    def ring_copy(d, i, part=0):
        block = pl.ds(0, half)
        if isinstance(i, int) and i == 0:
            block = pl.ds(gone, half - gone)
        elif isinstance(i, int) and i == steps - 1:
            block = pl.ds(half - width, width) if part else pl.ds(0, half - width)
        return pltpu.make_async_remote_copy(
            sendb.at[d, i, :, block], recvb.at[d, i, :, block], ring_send.at[d, i + part], ring_recv.at[d, i + part],
            device_id=(ring_to[d], sec), device_id_type=MESH)

    def term(k, h, s):
        return jnp.dot(xt[k], gv[:, pl.ds(pl.multiple_of(h * half + s * width, 128), width)], preferred_element_type=F32)

    def target(d, i):
        dist = n_chips // 2 - lax.div(i + 1, 2)
        return lax.rem(z + dist, n_chips) if d == 0 else lax.rem(z + n_chips - dist, n_chips)

    def cols(s):
        return slice(s * width, (s + 1) * width)

    def across(factor, n):
        return jnp.concatenate([factor] * (n // 128), axis=1)

    def step(i, add=True):
        for d in range(2):
            for s in range(PIECES):
                part = term(target(d, i), lax.rem(i + d, 2), s)
                if add:
                    if s == 0:
                        ring_copy(d, i - 2).wait_recv()
                    part += recvb[d, i - 2, :, cols(s)].astype(F32)
                sendb[d, i, :, cols(s)] = part.astype(BF16)
                if isinstance(i, int) and i == steps - 1 and s == PIECES - 2:
                    ring_copy(d, i).start()
            ring_copy(d, i, isinstance(i, int) and i == steps - 1).start()

    for d in range(2):
        for lo, hi in rest:
            own, other = (pre[d, e, :, lo - gone:hi - gone] * across(facs[e, 0:1], hi - lo) for e in range(2))
            sendb[d, 0, :, lo:hi] = (own + other).astype(BF16)
        ring_copy(d, 0).start()
    for k in (1, 2):
        xb_swap(owner(k)).start()
    for h in range(2):
        g_swap(h, 0).start()
    for d in range(2):
        up_copy(d).start()

    @pl.loop(3, n_chips)
    def _(k):
        xb_swap(owner(k)).start()

    @pl.loop(1, 3)
    def _(k):
        turn(owner(k))
        scale(owner(k))

    for h in range(2):
        g_swap(h, 0).wait_recv()
    step(1, add=False)

    @pl.loop(3, n_chips)
    def _(k):
        turn(owner(k))
        scale(owner(k))

    for d in range(2):
        for s in range(PIECES):
            part = term(target(d, 2), d, s)
            if s == 0:
                up_copy(d).wait_recv()
            if s < EARLY:
                for e in range(2):
                    early_wait(d, s, e)
                    part += recvu[d, s, e].astype(F32) * across(upfac[d, e, 0:1], width)
            else:
                if s == EARLY:
                    ring_copy(d, 0).wait_recv()
                part += recvb[d, 0, :, cols(s)].astype(F32)
            sendb[d, 2, :, cols(s)] = part.astype(BF16)
        ring_copy(d, 2).start()

    @pl.loop(3, steps - 1)
    def _(i):
        step(i)

    step(steps - 1)

    for d in range(2):
        for s in range(PIECES):
            part = term(z, d, s)
            if s == 0:
                ring_copy(1 - d, steps - 2).wait_recv()
            fin[d * PIECES + s] = part + recvb[1 - d, steps - 2, :, cols(s)].astype(F32)

    for s in range(PIECES):
        for d in range(2):
            c = d * PIECES + s
            if s == 0 or s == PIECES - 1:
                ring_copy(d, steps - 1, int(s > 0)).wait_recv()
            done = (fin[c] + recvb[d, steps - 1, :, cols(s)].astype(F32)) * weight
            out_ref[:, cols(c)] = done.astype(out_ref.dtype)

    len_swap.wait_send()
    for d in range(2):
        up_copy(d).wait_send()
        for e in range(2):
            for p in range(EARLY):
                early_copy(d, p, e).wait_send()
            g_swap(d, e).wait_send()
        for i in range(steps):
            ring_copy(d, i).wait_send()
        ring_copy(d, steps - 1, 1).wait_send()
    for j in range(side):
        col_copy(1, j, sec_y).wait_send()
        if j:
            row_copy(j, sec_x).wait_send()
            col_copy(0, j, sec_y).wait_send()

    @pl.loop(0, n_chips)
    def _(k):
        xb_swap(k).wait_send()


def shards(layer_inputs, output_grads, lengths):
    n_dp, n_sec = lax.axis_size("dp"), lax.axis_size("section")
    inputs = layer_inputs[0, 0]
    grads = output_grads[0, 0]
    seq, din = inputs.shape
    dout = grads.shape[1]
    rows = din // n_dp
    n_chips = n_dp // 2
    steps = n_chips - 1
    half = dout // 2
    width = half // PIECES
    side = math.isqrt(n_sec)
    weight = math.sqrt(din * dout * n_sec / n_dp)
    dma = pltpu.SemaphoreType.DMA
    vmem = pltpu.VMEM
    out = pl.pallas_call(
        functools.partial(kernel, (n_chips, side, rows), weight),
        out_shape=jax.ShapeDtypeStruct((rows, dout), BF16),
        in_specs=[
            pl.BlockSpec(memory_space=pltpu.SMEM),
            pl.BlockSpec(memory_space=pl.ANY),
            pl.BlockSpec(memory_space=pl.ANY),
        ],
        out_specs=pl.BlockSpec(memory_space=pltpu.VMEM),
        scratch_shapes=dict(
            xe=vmem((seq, 2 * rows), BF16),
            xv=vmem((seq, din), BF16),
            xb=vmem((n_chips, seq, rows), BF16),
            gv=vmem((2 * seq, dout), BF16),
            xt=vmem((n_chips, rows, 2 * seq), BF16),
            sendb=vmem((2, steps, rows, half), BF16),
            recvb=vmem((2, steps, rows, half), BF16),
            sendu=vmem((2, EARLY, 2, rows, width), BF16),
            recvu=vmem((2, EARLY, 2, rows, width), BF16),
            pre=vmem((2, 2, rows, (PIECES - EARLY) * width), F32),
            fin=vmem((2 * PIECES, rows, width), F32),
            gin=vmem((seq, seq), F32),
            gout=vmem((seq, seq), F32),
            row_tile=vmem((8, 128), F32),
            col_tile=vmem((8, 128), F32),
            rows_in=vmem((side, 8, 128), F32),
            cols_in=vmem((2, side, 8, 128), F32),
            lens=vmem((2, 8, 128), F32),
            facs=vmem((2, 8, 128), F32),
            upfac=vmem((2, 2, 8, 128), F32),
            xe_sem=dma,
            xv_sem=dma,
            g_sem=dma((2, 2)),
            xb_send=dma((n_chips,)),
            xb_recv=dma((n_chips,)),
            g_send=dma((2, 2)),
            g_recv=dma((2, 2)),
            len_sem=dma((2,)),
            row_send=dma((side,)),
            row_recv=dma((side,)),
            col_send=dma((2, side)),
            col_recv=dma((2, side)),
            early_send=dma((2, EARLY, 2)),
            early_recv=dma((2, EARLY, 2)),
            up_send=dma((2,)),
            up_recv=dma((2,)),
            ring_send=dma((2, steps + 1)),
            ring_recv=dma((2, steps + 1)),
        ),
        compiler_params=pltpu.CompilerParams(
            collective_id=0, has_side_effects=True, vmem_limit_bytes=52 * 2**20
        ),
        cost_estimate=pl.CostEstimate(
            flops=2 * seq * din * dout + 2 * seq * seq * (din + dout), bytes_accessed=2 * seq * (din + dout),
            transcendentals=0,
        ),
    )(lengths, inputs, grads)
    return out[None]


def solution(mesh):
    placed = (P("section", "dp", None, None), P("section", "dp", None, None), P("dp"))
    return jax.shard_map(
        shards, mesh=mesh, in_specs=placed, out_specs=P("section", "dp", None), check_vma=False
    )
```

```python
import functools
import math

import jax
import jax.numpy as jnp
from jax import lax
from jax.experimental import pallas as pl
from jax.experimental.pallas import tpu as pltpu
from jax.sharding import PartitionSpec as P

F32 = jnp.float32
BF16 = jnp.bfloat16
MESH = pl.DeviceIdType.MESH
PIECES = 3
EARLY = 2
PART = 512


def kernel(dims, weight, len_ref, x_ref, g_ref, out_ref, xe, xv, xb, gv, xt, sendb, recvb, sendu, recvu, pre, fin, gin, gout,
           row_tile, col_tile, rows_in, cols_in, lens, facs, upfac, xe_sem, xv_sem, g_sem, xb_send, xb_recv, g_send, g_recv,
           len_sem, row_send, row_recv, col_send, col_recv, early_send, early_recv, up_send, up_recv, ring_send, ring_recv):
    n_chips, side, rows = dims
    seq = x_ref.shape[0]
    half = sendb.shape[3]
    width = half // PIECES
    gone = EARLY * PART
    mid = seq // 2
    steps = n_chips - 1
    dp = lax.axis_index("dp")
    sec = lax.axis_index("section")
    z = lax.div(dp, 2)
    core = lax.rem(dp, 2)
    partner = dp + 1 - 2 * core
    ahead = lax.rem(dp + 2, 2 * n_chips)
    behind = lax.rem(dp + 2 * n_chips - 2, 2 * n_chips)
    ring_to = (ahead, behind)
    sec_x = lax.div(sec, side)
    sec_y = lax.rem(sec, side)

    def in_row(j):
        return lax.rem(sec_x + j, side) * side + sec_y

    def in_col(j):
        return sec_x * side + lax.rem(sec_y + j, side)

    def owner(k):
        far = lax.div(k + 1, 2)
        turn = jnp.where(lax.rem(k, 2) == 1, n_chips - far, far)
        return lax.rem(z + n_chips // 2 + turn, n_chips)

    def x_cols(k, c):
        return pl.ds(pl.multiple_of((2 * k + c) * rows, 128), rows)

    def g_cols(h, part):
        return pl.ds(h * half + gone, half - gone) if part else pl.ds(h * half, gone)

    def g_copy(h, part):
        cols = g_cols(h, part)
        return pltpu.make_async_copy(g_ref.at[:, cols], gv.at[pl.ds(0, seq), cols], g_sem.at[h, part])

    def g_swap(h, part):
        cols = g_cols(h, part)
        return pltpu.make_async_remote_copy(
            g_ref.at[:, cols], gv.at[pl.ds(seq, seq), cols], g_send.at[h, part], g_recv.at[h, part],
            device_id=(partner, sec), device_id_type=MESH)

    def xb_swap(k):
        return pltpu.make_async_remote_copy(
            x_ref.at[:, x_cols(k, 1 - core)], xb.at[k], xb_send.at[k], xb_recv.at[k],
            device_id=(partner, sec), device_id_type=MESH)

    first = owner(0)
    xe_cols = pl.ds(pl.multiple_of(2 * first * rows, 128), 2 * rows)
    xe_copy = pltpu.make_async_copy(x_ref.at[:, xe_cols], xe, xe_sem)
    x_copy = pltpu.make_async_copy(x_ref, xv, xv_sem)
    xe_copy.start()
    for h in range(2):
        g_copy(h, 0).start()
    x_copy.start()
    for h in range(2):
        g_copy(h, 1).start()

    barrier = pltpu.get_barrier_semaphore()
    peers = [(peer + other, sec) for peer in ring_to for other in (0, partner - dp)]
    peers += [(dp, in_row(j)) for j in range(1, side)] + [(dp, in_col(j)) for j in range(1, side)]
    peers += [(partner, in_col(j)) for j in range(side)]
    for peer in peers:
        pl.semaphore_signal(barrier, inc=1, device_id=peer, device_id_type=MESH)

    xe_copy.wait()
    token = lax.broadcasted_iota(jnp.int32, xe.shape, 0)
    xet = jnp.where(token < len_ref[0], xe[...].astype(F32), 0.0).T.astype(BF16)

    def early_copy(d, p, e):
        slot = lax.rem(core + e, 2)
        return pltpu.make_async_remote_copy(
            sendu.at[d, p, e], recvu.at[d, p, slot], early_send.at[d, p, e], early_recv.at[d, p, slot],
            device_id=(ring_to[d] - core + e, sec), device_id_type=MESH)

    def early_wait(d, p, slot):
        pltpu.make_async_remote_copy(
            sendu.at[d, p, slot], recvu.at[d, p, slot], early_send.at[d, p, slot], early_recv.at[d, p, slot],
            device_id=(ring_to[d], sec), device_id_type=MESH).wait_recv()

    def early_terms(p):
        for d in range(2):
            if p == 0:
                g_copy(d, 0).wait()
            lo = d * half + p * PART
            early = jnp.dot(xet, gv[:seq, lo:lo + PART], preferred_element_type=F32).astype(BF16)
            for e in range(2):
                sendu[d, p, e] = early[e * rows:(e + 1) * rows]

    def early_start(p):
        for e in range(2):
            for d in range(2):
                early_copy(d, p, e).start()

    early_terms(0)
    lens[0] = jnp.full(lens.shape[1:], len_ref[0], F32)
    pl.semaphore_wait(barrier, len(peers))
    early_start(0)
    len_swap = pltpu.make_async_remote_copy(
        lens.at[0], lens.at[1], len_sem.at[0], len_sem.at[1], device_id=(partner, sec), device_id_type=MESH)
    len_swap.start()
    xb_swap(first).start()
    for h in range(2):
        g_swap(h, 1).start()

    def gram(acc, block, new=False):
        nt = (((1,), (1,)), ((), ()))
        left = lax.dot_general(block[:mid], block[:mid], nt, preferred_element_type=F32)
        right = lax.dot_general(block, block[mid:], nt, preferred_element_type=F32)
        if new:
            acc[:mid, :mid] = left
            acc[:, mid:] = right
        else:
            acc[:mid, :mid] += left
            acc[:, mid:] += right

    x_copy.wait()
    gram(gin, xv[...], True)
    for p in range(1, EARLY):
        early_terms(p)
        early_start(p)
    for h in range(2):
        g_copy(h, 1).wait()
        gram(gout, gv[:seq, h * half:(h + 1) * half], h == 0)

    row = lax.broadcasted_iota(jnp.int32, (seq, mid), 0)
    col = lax.broadcasted_iota(jnp.int32, (seq, mid), 1)
    n_live = len_ref[0]
    left_live = (row[:mid] < n_live) & (col[:mid] < n_live)
    left = jnp.where(left_live, gin[:mid, :mid] * gout[:mid, :mid], 0.0)
    twice = jnp.where(row < mid, 2.0, 1.0)
    right_live = (row < n_live) & (col + mid < n_live)
    right = jnp.where(right_live, gin[:, mid:] * gout[:, mid:] * twice, 0.0)
    cells = left + right[:mid] + right[mid:]
    norm = jnp.sum(jnp.sum(cells, axis=0, keepdims=True), axis=1, keepdims=True)
    row_tile[...] = jnp.broadcast_to(norm, row_tile.shape)

    def row_copy(j, frm):
        return pltpu.make_async_remote_copy(
            row_tile, rows_in.at[frm], row_send.at[j], row_recv.at[frm], device_id=(dp, in_row(j)), device_id_type=MESH)

    def col_copy(e, j, frm):
        return pltpu.make_async_remote_copy(
            col_tile, cols_in.at[e, frm], col_send.at[e, j], col_recv.at[e, frm],
            device_id=(partner if e else dp, in_col(j)), device_id_type=MESH)

    for j in range(1, side):
        row_copy(j, sec_x).start()
    rows_in[sec_x] = row_tile[...]

    token = lax.broadcasted_iota(jnp.int32, (seq, rows), 0).astype(F32)

    def turn(k):
        xb_swap(k).wait_recv()
        for e, block in enumerate((xv[:, x_cols(k, core)], xb[k])):
            block = jnp.where(token < lens[e, 0:1, :], block.astype(F32), 0.0)
            xt[k, :, e * seq:(e + 1) * seq] = block.T.astype(BF16)

    def scale(k):
        for e in range(2):
            factor = facs[e, 0:1, :]
            for j in range(seq // 128):
                cols = slice(e * seq + j * 128, e * seq + (j + 1) * 128)
                xt[k, :, cols] = (xt[k, :, cols].astype(F32) * factor).astype(BF16)

    for j in range(1, side):
        row_copy(j, lax.rem(sec_x + j, side)).wait_recv()
    col_tile[...] = jnp.sum(rows_in[...], axis=0)
    for j in range(side):
        col_copy(1, j, sec_y).start()
        if j:
            col_copy(0, j, sec_y).start()
    cols_in[0, sec_y] = col_tile[...]

    len_swap.wait_recv()
    turn(first)
    rest = [(lo, min(lo + width, half)) for lo in range(gone, half, width)]
    for d in range(2):
        g_swap(d, 1).wait_recv()
        for lo, hi in rest:
            for e in range(2):
                tokens = slice(e * seq, (e + 1) * seq)
                pre[d, e, :, lo - gone:hi - gone] = jnp.dot(
                    xt[first, :, tokens], gv[tokens, d * half + lo:d * half + hi], preferred_element_type=F32)

    for j in range(side):
        frm = lax.rem(sec_y + j, side)
        col_copy(1, j, frm).wait_recv()
        if j:
            col_copy(0, j, frm).wait_recv()
    for e in range(2):
        facs[e] = jnp.minimum(1.0, 1.0 / jnp.sqrt(jnp.sum(cols_in[e], axis=0) + 1e-06))

    def up_copy(d):
        return pltpu.make_async_remote_copy(
            facs, upfac.at[d], up_send.at[d], up_recv.at[d], device_id=(ring_to[d], sec), device_id_type=MESH)

    def ring_copy(d, i, part=0):
        block = pl.ds(0, half)
        if isinstance(i, int) and i == 0:
            block = pl.ds(gone, half - gone)
        elif isinstance(i, int) and i == steps - 1:
            block = pl.ds(half - width, width) if part else pl.ds(0, half - width)
        return pltpu.make_async_remote_copy(
            sendb.at[d, i, :, block], recvb.at[d, i, :, block], ring_send.at[d, i + part], ring_recv.at[d, i + part],
            device_id=(ring_to[d], sec), device_id_type=MESH)

    def term(k, h, s):
        return jnp.dot(xt[k], gv[:, pl.ds(pl.multiple_of(h * half + s * width, 128), width)], preferred_element_type=F32)

    def target(d, i):
        dist = n_chips // 2 - lax.div(i + 1, 2)
        return lax.rem(z + dist, n_chips) if d == 0 else lax.rem(z + n_chips - dist, n_chips)

    def cols(s):
        return slice(s * width, (s + 1) * width)

    def across(factor, n):
        return jnp.concatenate([factor] * (n // 128), axis=1)

    def step(i, add=True):
        for d in range(2):
            for s in range(PIECES):
                part = term(target(d, i), lax.rem(i + d, 2), s)
                if add:
                    if s == 0:
                        ring_copy(d, i - 2).wait_recv()
                    part += recvb[d, i - 2, :, cols(s)].astype(F32)
                sendb[d, i, :, cols(s)] = part.astype(BF16)
                if isinstance(i, int) and i == steps - 1 and s == PIECES - 2:
                    ring_copy(d, i).start()
            ring_copy(d, i, isinstance(i, int) and i == steps - 1).start()

    for d in range(2):
        for lo, hi in rest:
            own, other = (pre[d, e, :, lo - gone:hi - gone] * across(facs[e, 0:1], hi - lo) for e in range(2))
            sendb[d, 0, :, lo:hi] = (own + other).astype(BF16)
        ring_copy(d, 0).start()
    for k in (1, 2):
        xb_swap(owner(k)).start()
    for h in range(2):
        g_swap(h, 0).start()
    for d in range(2):
        up_copy(d).start()

    @pl.loop(3, n_chips)
    def _(k):
        xb_swap(owner(k)).start()

    @pl.loop(1, 3)
    def _(k):
        turn(owner(k))
        scale(owner(k))

    for h in range(2):
        g_swap(h, 0).wait_recv()
    step(1, add=False)

    @pl.loop(3, n_chips)
    def _(k):
        turn(owner(k))
        scale(owner(k))

    for d in range(2):
        up_copy(d).wait_recv()
        for p in range(EARLY):
            lo, hi = p * PART, (p + 1) * PART
            part = jnp.dot(xt[target(d, 2)], gv[:, d * half + lo:d * half + hi], preferred_element_type=F32)
            for e in range(2):
                early_wait(d, p, e)
                part += recvu[d, p, e].astype(F32) * across(upfac[d, e, 0:1], PART)
            sendb[d, 2, :, lo:hi] = part.astype(BF16)
        for lo, hi in rest:
            part = jnp.dot(xt[target(d, 2)], gv[:, d * half + lo:d * half + hi], preferred_element_type=F32)
            if lo == gone:
                ring_copy(d, 0).wait_recv()
            sendb[d, 2, :, lo:hi] = (part + recvb[d, 0, :, lo:hi].astype(F32)).astype(BF16)
        ring_copy(d, 2).start()

    @pl.loop(3, steps - 1)
    def _(i):
        step(i)

    step(steps - 1)

    for d in range(2):
        for s in range(PIECES):
            part = term(z, d, s)
            if s == 0:
                ring_copy(1 - d, steps - 2).wait_recv()
            fin[d * PIECES + s] = part + recvb[1 - d, steps - 2, :, cols(s)].astype(F32)

    for s in range(PIECES):
        for d in range(2):
            c = d * PIECES + s
            if s == 0 or s == PIECES - 1:
                ring_copy(d, steps - 1, int(s > 0)).wait_recv()
            done = (fin[c] + recvb[d, steps - 1, :, cols(s)].astype(F32)) * weight
            out_ref[:, cols(c)] = done.astype(out_ref.dtype)

    len_swap.wait_send()
    for d in range(2):
        up_copy(d).wait_send()
        for e in range(2):
            for p in range(EARLY):
                early_copy(d, p, e).wait_send()
            g_swap(d, e).wait_send()
        for i in range(steps):
            ring_copy(d, i).wait_send()
        ring_copy(d, steps - 1, 1).wait_send()
    for j in range(side):
        col_copy(1, j, sec_y).wait_send()
        if j:
            row_copy(j, sec_x).wait_send()
            col_copy(0, j, sec_y).wait_send()

    @pl.loop(0, n_chips)
    def _(k):
        xb_swap(k).wait_send()


def shards(layer_inputs, output_grads, lengths):
    n_dp, n_sec = lax.axis_size("dp"), lax.axis_size("section")
    inputs = layer_inputs[0, 0]
    grads = output_grads[0, 0]
    seq, din = inputs.shape
    dout = grads.shape[1]
    rows = din // n_dp
    n_chips = n_dp // 2
    steps = n_chips - 1
    half = dout // 2
    width = half // PIECES
    side = math.isqrt(n_sec)
    weight = math.sqrt(din * dout * n_sec / n_dp)
    dma = pltpu.SemaphoreType.DMA
    vmem = pltpu.VMEM
    out = pl.pallas_call(
        functools.partial(kernel, (n_chips, side, rows), weight),
        out_shape=jax.ShapeDtypeStruct((rows, dout), BF16),
        in_specs=[
            pl.BlockSpec(memory_space=pltpu.SMEM),
            pl.BlockSpec(memory_space=pl.ANY),
            pl.BlockSpec(memory_space=pl.ANY),
        ],
        out_specs=pl.BlockSpec(memory_space=pltpu.VMEM),
        scratch_shapes=dict(
            xe=vmem((seq, 2 * rows), BF16),
            xv=vmem((seq, din), BF16),
            xb=vmem((n_chips, seq, rows), BF16),
            gv=vmem((2 * seq, dout), BF16),
            xt=vmem((n_chips, rows, 2 * seq), BF16),
            sendb=vmem((2, steps, rows, half), BF16),
            recvb=vmem((2, steps, rows, half), BF16),
            sendu=vmem((2, EARLY, 2, rows, PART), BF16),
            recvu=vmem((2, EARLY, 2, rows, PART), BF16),
            pre=vmem((2, 2, rows, half - EARLY * PART), F32),
            fin=vmem((2 * PIECES, rows, width), F32),
            gin=vmem((seq, seq), F32),
            gout=vmem((seq, seq), F32),
            row_tile=vmem((8, 128), F32),
            col_tile=vmem((8, 128), F32),
            rows_in=vmem((side, 8, 128), F32),
            cols_in=vmem((2, side, 8, 128), F32),
            lens=vmem((2, 8, 128), F32),
            facs=vmem((2, 8, 128), F32),
            upfac=vmem((2, 2, 8, 128), F32),
            xe_sem=dma,
            xv_sem=dma,
            g_sem=dma((2, 2)),
            xb_send=dma((n_chips,)),
            xb_recv=dma((n_chips,)),
            g_send=dma((2, 2)),
            g_recv=dma((2, 2)),
            len_sem=dma((2,)),
            row_send=dma((side,)),
            row_recv=dma((side,)),
            col_send=dma((2, side)),
            col_recv=dma((2, side)),
            early_send=dma((2, EARLY, 2)),
            early_recv=dma((2, EARLY, 2)),
            up_send=dma((2,)),
            up_recv=dma((2,)),
            ring_send=dma((2, steps + 1)),
            ring_recv=dma((2, steps + 1)),
        ),
        compiler_params=pltpu.CompilerParams(
            collective_id=0, has_side_effects=True, vmem_limit_bytes=52 * 2**20
        ),
        cost_estimate=pl.CostEstimate(
            flops=2 * seq * din * dout + 2 * seq * seq * (din + dout), bytes_accessed=2 * seq * (din + dout),
            transcendentals=0,
        ),
    )(lengths, inputs, grads)
    return out[None]


def solution(mesh):
    placed = (P("section", "dp", None, None), P("section", "dp", None, None), P("dp"))
    return jax.shard_map(
        shards, mesh=mesh, in_specs=placed, out_specs=P("section", "dp", None), check_vma=False
    )
```

```python
import functools
import math

import jax
import jax.numpy as jnp
from jax import lax
from jax.experimental import pallas as pl
from jax.experimental.pallas import tpu as pltpu
from jax.sharding import PartitionSpec as P

F32 = jnp.float32
BF16 = jnp.bfloat16
MESH = pl.DeviceIdType.MESH
PIECES = 3
EARLY = ((0, 512), (512, 896))


def kernel(dims, weight, len_ref, x_ref, g_ref, out_ref, xe, xv, xb, gv, xt, sendb, recvb, sendu, recvu, pre, fin, gin, gout,
           row_tile, col_tile, rows_in, cols_in, lens, facs, upfac, xe_sem, xv_sem, g_sem, xb_send, xb_recv, g_send, g_recv,
           len_sem, row_send, row_recv, col_send, col_recv, early_send, early_recv, up_send, up_recv, ring_send, ring_recv):
    n_chips, side, rows = dims
    seq = x_ref.shape[0]
    half = sendb.shape[3]
    width = half // PIECES
    gone = EARLY[-1][1]
    rest = ((gone, half - width), (half - width, half))
    mid = seq // 2
    steps = n_chips - 1
    dp = lax.axis_index("dp")
    sec = lax.axis_index("section")
    z = lax.div(dp, 2)
    core = lax.rem(dp, 2)
    partner = dp + 1 - 2 * core
    ahead = lax.rem(dp + 2, 2 * n_chips)
    behind = lax.rem(dp + 2 * n_chips - 2, 2 * n_chips)
    ring_to = (ahead, behind)
    sec_x = lax.div(sec, side)
    sec_y = lax.rem(sec, side)

    def in_row(j):
        return lax.rem(sec_x + j, side) * side + sec_y

    def in_col(j):
        return sec_x * side + lax.rem(sec_y + j, side)

    def owner(k):
        far = lax.div(k + 1, 2)
        turn = jnp.where(lax.rem(k, 2) == 1, n_chips - far, far)
        return lax.rem(z + n_chips // 2 + turn, n_chips)

    def x_cols(k, c):
        return pl.ds(pl.multiple_of((2 * k + c) * rows, 128), rows)

    def g_cols(h, part):
        return pl.ds(h * half + gone, half - gone) if part else pl.ds(h * half, gone)

    def g_copy(h, part):
        cols = g_cols(h, part)
        return pltpu.make_async_copy(g_ref.at[:, cols], gv.at[pl.ds(0, seq), cols], g_sem.at[h, part])

    def g_swap(h, part):
        cols = g_cols(h, part)
        return pltpu.make_async_remote_copy(
            g_ref.at[:, cols], gv.at[pl.ds(seq, seq), cols], g_send.at[h, part], g_recv.at[h, part],
            device_id=(partner, sec), device_id_type=MESH)

    def xb_swap(k):
        return pltpu.make_async_remote_copy(
            x_ref.at[:, x_cols(k, 1 - core)], xb.at[k], xb_send.at[k], xb_recv.at[k],
            device_id=(partner, sec), device_id_type=MESH)

    first = owner(0)
    xe_cols = pl.ds(pl.multiple_of(2 * first * rows, 128), 2 * rows)
    xe_copy = pltpu.make_async_copy(x_ref.at[:, xe_cols], xe, xe_sem)
    x_copy = pltpu.make_async_copy(x_ref, xv, xv_sem)
    xe_copy.start()
    for h in range(2):
        g_copy(h, 0).start()

    barrier = pltpu.get_barrier_semaphore()
    peers = [(peer + other, sec) for peer in ring_to for other in (0, partner - dp)]
    peers += [(dp, in_row(j)) for j in range(1, side)] + [(dp, in_col(j)) for j in range(1, side)]
    peers += [(partner, in_col(j)) for j in range(side)]
    for peer in peers:
        pl.semaphore_signal(barrier, inc=1, device_id=peer, device_id_type=MESH)
    x_copy.start()
    for h in range(2):
        g_copy(h, 1).start()

    xe_copy.wait()
    token = lax.broadcasted_iota(jnp.int32, xe.shape, 0)
    xet = jnp.where(token < len_ref[0], xe[...].astype(F32), 0.0).T.astype(BF16)

    def early_copy(d, p, e, slot):
        block = pl.ds(EARLY[p][0], EARLY[p][1] - EARLY[p][0])
        return pltpu.make_async_remote_copy(
            sendu.at[d, e, :, block], recvu.at[d, slot, :, block], early_send.at[d, p, e], early_recv.at[d, p, slot],
            device_id=(ring_to[d] - core + e, sec), device_id_type=MESH)

    def early_terms(p):
        for d in range(2):
            if p == 0:
                g_copy(d, 0).wait()
            lo, hi = EARLY[p]
            early = jnp.dot(xet, gv[:seq, d * half + lo:d * half + hi], preferred_element_type=F32).astype(BF16)
            for e in range(2):
                sendu[d, e, :, lo:hi] = early[e * rows:(e + 1) * rows]

    def early_start(p):
        for e in range(2):
            for d in range(2):
                early_copy(d, p, e, lax.rem(core + e, 2)).start()

    early_terms(0)
    lens[0] = jnp.full(lens.shape[1:], len_ref[0], F32)
    pl.semaphore_wait(barrier, len(peers))
    early_start(0)
    len_swap = pltpu.make_async_remote_copy(
        lens.at[0], lens.at[1], len_sem.at[0], len_sem.at[1], device_id=(partner, sec), device_id_type=MESH)
    len_swap.start()
    xb_swap(first).start()
    for h in range(2):
        g_swap(h, 1).start()

    def gram(acc, block, new=False):
        nt = (((1,), (1,)), ((), ()))
        left = lax.dot_general(block[:mid], block[:mid], nt, preferred_element_type=F32)
        right = lax.dot_general(block, block[mid:], nt, preferred_element_type=F32)
        if new:
            acc[:mid, :mid] = left
            acc[:, mid:] = right
        else:
            acc[:mid, :mid] += left
            acc[:, mid:] += right

    x_copy.wait()
    gram(gin, xv[...], True)
    for h in range(2):
        g_copy(h, 1).wait()
        gram(gout, gv[:seq, h * half:(h + 1) * half], h == 0)

    row = lax.broadcasted_iota(jnp.int32, (seq, mid), 0)
    col = lax.broadcasted_iota(jnp.int32, (seq, mid), 1)
    n_live = len_ref[0]
    left_live = (row[:mid] < n_live) & (col[:mid] < n_live)
    left = jnp.where(left_live, gin[:mid, :mid] * gout[:mid, :mid], 0.0)
    twice = jnp.where(row < mid, 2.0, 1.0)
    right_live = (row < n_live) & (col + mid < n_live)
    right = jnp.where(right_live, gin[:, mid:] * gout[:, mid:] * twice, 0.0)
    cells = left + right[:mid] + right[mid:]
    norm = jnp.sum(jnp.sum(cells, axis=0, keepdims=True), axis=1, keepdims=True)
    row_tile[...] = jnp.broadcast_to(norm, row_tile.shape)

    def row_copy(j, frm):
        return pltpu.make_async_remote_copy(
            row_tile, rows_in.at[frm], row_send.at[j], row_recv.at[frm], device_id=(dp, in_row(j)), device_id_type=MESH)

    def col_copy(e, j, frm):
        return pltpu.make_async_remote_copy(
            col_tile, cols_in.at[e, frm], col_send.at[e, j], col_recv.at[e, frm],
            device_id=(partner if e else dp, in_col(j)), device_id_type=MESH)

    for j in range(1, side):
        row_copy(j, sec_x).start()
    rows_in[sec_x] = row_tile[...]
    for p in range(1, len(EARLY)):
        early_terms(p)
        early_start(p)

    token = lax.broadcasted_iota(jnp.int32, (seq, rows), 0).astype(F32)

    def turn(k):
        xb_swap(k).wait_recv()
        for e, block in enumerate((xv[:, x_cols(k, core)], xb[k])):
            block = jnp.where(token < lens[e, 0:1, :], block.astype(F32), 0.0)
            xt[k, :, e * seq:(e + 1) * seq] = block.T.astype(BF16)

    def scale(k):
        for e in range(2):
            factor = facs[e, 0:1, :]
            for j in range(seq // 128):
                cols = slice(e * seq + j * 128, e * seq + (j + 1) * 128)
                xt[k, :, cols] = (xt[k, :, cols].astype(F32) * factor).astype(BF16)

    for j in range(1, side):
        row_copy(j, lax.rem(sec_x + j, side)).wait_recv()
    col_tile[...] = jnp.sum(rows_in[...], axis=0)
    for j in range(side):
        col_copy(1, j, sec_y).start()
        if j:
            col_copy(0, j, sec_y).start()
    cols_in[0, sec_y] = col_tile[...]

    len_swap.wait_recv()
    turn(first)
    lo, hi = rest[0]
    for d in range(2):
        g_swap(d, 1).wait_recv()
        for e in range(2):
            tokens = slice(e * seq, (e + 1) * seq)
            pre[d, e] = jnp.dot(
                xt[first, :, tokens], gv[tokens, d * half + lo:d * half + hi], preferred_element_type=F32)

    for j in range(side):
        frm = lax.rem(sec_y + j, side)
        col_copy(1, j, frm).wait_recv()
        if j:
            col_copy(0, j, frm).wait_recv()
    for e in range(2):
        facs[e] = jnp.minimum(1.0, 1.0 / jnp.sqrt(jnp.sum(cols_in[e], axis=0) + 1e-06))

    def up_copy(d):
        return pltpu.make_async_remote_copy(
            facs, upfac.at[d], up_send.at[d], up_recv.at[d], device_id=(ring_to[d], sec), device_id_type=MESH)

    def ring_copy(d, i, part=0):
        block = pl.ds(0, half)
        sem = i + part
        if isinstance(i, int) and i == 0:
            block = pl.ds(rest[part][0], rest[part][1] - rest[part][0])
            sem = part * (steps + 1)
        elif isinstance(i, int) and i == steps - 1:
            block = pl.ds(half - width, width) if part else pl.ds(0, half - width)
        return pltpu.make_async_remote_copy(
            sendb.at[d, i, :, block], recvb.at[d, i, :, block], ring_send.at[d, sem], ring_recv.at[d, sem],
            device_id=(ring_to[d], sec), device_id_type=MESH)

    def term(k, h, s):
        return jnp.dot(xt[k], gv[:, pl.ds(pl.multiple_of(h * half + s * width, 128), width)], preferred_element_type=F32)

    def target(d, i):
        dist = n_chips // 2 - lax.div(i + 1, 2)
        return lax.rem(z + dist, n_chips) if d == 0 else lax.rem(z + n_chips - dist, n_chips)

    def cols(s):
        return slice(s * width, (s + 1) * width)

    def across(factor, n):
        return jnp.concatenate([factor] * (n // 128), axis=1)

    def step(i, add=True):
        for d in range(2):
            for s in range(PIECES):
                part = term(target(d, i), lax.rem(i + d, 2), s)
                if add:
                    if s == 0:
                        ring_copy(d, i - 2).wait_recv()
                    part += recvb[d, i - 2, :, cols(s)].astype(F32)
                sendb[d, i, :, cols(s)] = part.astype(BF16)
                if isinstance(i, int) and i == steps - 1 and s == PIECES - 2:
                    ring_copy(d, i).start()
            ring_copy(d, i, isinstance(i, int) and i == steps - 1).start()

    lo, hi = rest[0]
    for d in range(2):
        own, other = (pre[d, e] * across(facs[e, 0:1], hi - lo) for e in range(2))
        sendb[d, 0, :, lo:hi] = (own + other).astype(BF16)
        ring_copy(d, 0).start()
    scale(first)
    lo, hi = rest[1]
    for d in range(2):
        part = jnp.dot(xt[first], gv[:, d * half + lo:d * half + hi], preferred_element_type=F32)
        sendb[d, 0, :, lo:hi] = part.astype(BF16)
        ring_copy(d, 0, 1).start()
    for k in (1, 2):
        xb_swap(owner(k)).start()
    for h in range(2):
        g_swap(h, 0).start()
    for d in range(2):
        up_copy(d).start()

    @pl.loop(3, n_chips)
    def _(k):
        xb_swap(owner(k)).start()

    @pl.loop(1, 3)
    def _(k):
        turn(owner(k))
        scale(owner(k))

    for h in range(2):
        g_swap(h, 0).wait_recv()
    step(1, add=False)

    @pl.loop(3, n_chips)
    def _(k):
        turn(owner(k))
        scale(owner(k))

    for d in range(2):
        up_copy(d).wait_recv()
        for p, (lo, hi) in enumerate(EARLY):
            part = jnp.dot(xt[target(d, 2)], gv[:, d * half + lo:d * half + hi], preferred_element_type=F32)
            for e in range(2):
                early_copy(d, p, e, e).wait_recv()
                part += recvu[d, e, :, lo:hi].astype(F32) * across(upfac[d, e, 0:1], hi - lo)
            sendb[d, 2, :, lo:hi] = part.astype(BF16)
        for p, (lo, hi) in enumerate(rest):
            part = jnp.dot(xt[target(d, 2)], gv[:, d * half + lo:d * half + hi], preferred_element_type=F32)
            ring_copy(d, 0, p).wait_recv()
            sendb[d, 2, :, lo:hi] = (part + recvb[d, 0, :, lo:hi].astype(F32)).astype(BF16)
        ring_copy(d, 2).start()

    @pl.loop(3, steps - 1)
    def _(i):
        step(i)

    step(steps - 1)

    for d in range(2):
        for s in range(PIECES):
            part = term(z, d, s)
            if s == 0:
                ring_copy(1 - d, steps - 2).wait_recv()
            fin[d * PIECES + s] = part + recvb[1 - d, steps - 2, :, cols(s)].astype(F32)

    for s in range(PIECES):
        for d in range(2):
            c = d * PIECES + s
            if s == 0 or s == PIECES - 1:
                ring_copy(d, steps - 1, int(s > 0)).wait_recv()
            done = (fin[c] + recvb[d, steps - 1, :, cols(s)].astype(F32)) * weight
            out_ref[:, cols(c)] = done.astype(out_ref.dtype)

    len_swap.wait_send()
    for d in range(2):
        up_copy(d).wait_send()
        for e in range(2):
            for p in range(len(EARLY)):
                early_copy(d, p, e, e).wait_send()
            g_swap(d, e).wait_send()
        for i in range(steps):
            ring_copy(d, i).wait_send()
        for i in (0, steps - 1):
            ring_copy(d, i, 1).wait_send()
    for j in range(side):
        col_copy(1, j, sec_y).wait_send()
        if j:
            row_copy(j, sec_x).wait_send()
            col_copy(0, j, sec_y).wait_send()

    @pl.loop(0, n_chips)
    def _(k):
        xb_swap(k).wait_send()


def shards(layer_inputs, output_grads, lengths):
    n_dp, n_sec = lax.axis_size("dp"), lax.axis_size("section")
    inputs = layer_inputs[0, 0]
    grads = output_grads[0, 0]
    seq, din = inputs.shape
    dout = grads.shape[1]
    rows = din // n_dp
    n_chips = n_dp // 2
    steps = n_chips - 1
    half = dout // 2
    width = half // PIECES
    side = math.isqrt(n_sec)
    gone = EARLY[-1][1]
    weight = math.sqrt(din * dout * n_sec / n_dp)
    dma = pltpu.SemaphoreType.DMA
    vmem = pltpu.VMEM
    out = pl.pallas_call(
        functools.partial(kernel, (n_chips, side, rows), weight),
        out_shape=jax.ShapeDtypeStruct((rows, dout), BF16),
        in_specs=[
            pl.BlockSpec(memory_space=pltpu.SMEM),
            pl.BlockSpec(memory_space=pl.ANY),
            pl.BlockSpec(memory_space=pl.ANY),
        ],
        out_specs=pl.BlockSpec(memory_space=pltpu.VMEM),
        scratch_shapes=dict(
            xe=vmem((seq, 2 * rows), BF16),
            xv=vmem((seq, din), BF16),
            xb=vmem((n_chips, seq, rows), BF16),
            gv=vmem((2 * seq, dout), BF16),
            xt=vmem((n_chips, rows, 2 * seq), BF16),
            sendb=vmem((2, steps, rows, half), BF16),
            recvb=vmem((2, steps, rows, half), BF16),
            sendu=vmem((2, 2, rows, gone), BF16),
            recvu=vmem((2, 2, rows, gone), BF16),
            pre=vmem((2, 2, rows, half - width - gone), F32),
            fin=vmem((2 * PIECES, rows, width), F32),
            gin=vmem((seq, seq), F32),
            gout=vmem((seq, seq), F32),
            row_tile=vmem((8, 128), F32),
            col_tile=vmem((8, 128), F32),
            rows_in=vmem((side, 8, 128), F32),
            cols_in=vmem((2, side, 8, 128), F32),
            lens=vmem((2, 8, 128), F32),
            facs=vmem((2, 8, 128), F32),
            upfac=vmem((2, 2, 8, 128), F32),
            xe_sem=dma,
            xv_sem=dma,
            g_sem=dma((2, 2)),
            xb_send=dma((n_chips,)),
            xb_recv=dma((n_chips,)),
            g_send=dma((2, 2)),
            g_recv=dma((2, 2)),
            len_sem=dma((2,)),
            row_send=dma((side,)),
            row_recv=dma((side,)),
            col_send=dma((2, side)),
            col_recv=dma((2, side)),
            early_send=dma((2, len(EARLY), 2)),
            early_recv=dma((2, len(EARLY), 2)),
            up_send=dma((2,)),
            up_recv=dma((2,)),
            ring_send=dma((2, steps + 2)),
            ring_recv=dma((2, steps + 2)),
        ),
        compiler_params=pltpu.CompilerParams(
            collective_id=0, has_side_effects=True, vmem_limit_bytes=52 * 2**20
        ),
        cost_estimate=pl.CostEstimate(
            flops=2 * seq * din * dout + 2 * seq * seq * (din + dout), bytes_accessed=2 * seq * (din + dout),
            transcendentals=0,
        ),
    )(lengths, inputs, grads)
    return out[None]


def solution(mesh):
    placed = (P("section", "dp", None, None), P("section", "dp", None, None), P("dp"))
    return jax.shard_map(
        shards, mesh=mesh, in_specs=placed, out_specs=P("section", "dp", None), check_vma=False
    )
```

```python
import functools
import math

import jax
import jax.numpy as jnp
from jax import lax
from jax.experimental import pallas as pl
from jax.experimental.pallas import tpu as pltpu
from jax.sharding import PartitionSpec as P

F32 = jnp.float32
BF16 = jnp.bfloat16
MESH = pl.DeviceIdType.MESH
PIECES = 3
EARLY = 2
PART = 512


def kernel(dims, weight, len_ref, x_ref, g_ref, out_ref, xe, xv, xb, gv, xt, sendb, recvb, sendu, recvu, pre, fin, gin, gout,
           row_tile, col_tile, rows_in, cols_in, lens, facs, upfac, xe_sem, xv_sem, g_sem, xb_send, xb_recv, g_send, g_recv,
           len_sem, row_send, row_recv, col_send, col_recv, early_send, early_recv, up_send, up_recv, ring_send, ring_recv):
    n_chips, side, rows = dims
    seq = x_ref.shape[0]
    half = sendb.shape[3]
    width = half // PIECES
    gone = EARLY * PART
    mid = seq // 2
    steps = n_chips - 1
    dp = lax.axis_index("dp")
    sec = lax.axis_index("section")
    z = lax.div(dp, 2)
    core = lax.rem(dp, 2)
    partner = dp + 1 - 2 * core
    ahead = lax.rem(dp + 2, 2 * n_chips)
    behind = lax.rem(dp + 2 * n_chips - 2, 2 * n_chips)
    ring_to = (ahead, behind)
    sec_x = lax.div(sec, side)
    sec_y = lax.rem(sec, side)

    def in_row(j):
        return lax.rem(sec_x + j, side) * side + sec_y

    def in_col(j):
        return sec_x * side + lax.rem(sec_y + j, side)

    def owner(k):
        far = lax.div(k + 1, 2)
        turn = jnp.where(lax.rem(k, 2) == 1, n_chips - far, far)
        return lax.rem(z + n_chips // 2 + turn, n_chips)

    def x_cols(k, c):
        return pl.ds(pl.multiple_of((2 * k + c) * rows, 128), rows)

    def g_cols(h, part):
        return pl.ds(h * half + gone, half - gone) if part else pl.ds(h * half, gone)

    def g_copy(h, part):
        cols = g_cols(h, part)
        return pltpu.make_async_copy(g_ref.at[:, cols], gv.at[pl.ds(0, seq), cols], g_sem.at[h, part])

    def g_swap(h, part):
        cols = g_cols(h, part)
        return pltpu.make_async_remote_copy(
            g_ref.at[:, cols], gv.at[pl.ds(seq, seq), cols], g_send.at[h, part], g_recv.at[h, part],
            device_id=(partner, sec), device_id_type=MESH)

    def xb_swap(k):
        return pltpu.make_async_remote_copy(
            x_ref.at[:, x_cols(k, 1 - core)], xb.at[k], xb_send.at[k], xb_recv.at[k],
            device_id=(partner, sec), device_id_type=MESH)

    first = owner(0)
    xe_cols = pl.ds(pl.multiple_of(2 * first * rows, 128), 2 * rows)
    xe_copy = pltpu.make_async_copy(x_ref.at[:, xe_cols], xe, xe_sem)
    x_copy = pltpu.make_async_copy(x_ref, xv, xv_sem)
    xe_copy.start()
    for h in range(2):
        g_copy(h, 0).start()
    x_copy.start()
    for h in range(2):
        g_copy(h, 1).start()

    barrier = pltpu.get_barrier_semaphore()
    peers = [(peer + other, sec) for peer in ring_to for other in (0, partner - dp)]
    peers += [(dp, in_row(j)) for j in range(1, side)] + [(dp, in_col(j)) for j in range(1, side)]
    peers += [(partner, in_col(j)) for j in range(side)]
    for peer in peers:
        pl.semaphore_signal(barrier, inc=1, device_id=peer, device_id_type=MESH)

    xe_copy.wait()
    token = lax.broadcasted_iota(jnp.int32, xe.shape, 0)
    xet = jnp.where(token < len_ref[0], xe[...].astype(F32), 0.0).T.astype(BF16)

    def early_copy(d, p, e):
        slot = lax.rem(core + e, 2)
        return pltpu.make_async_remote_copy(
            sendu.at[d, p, e], recvu.at[d, p, slot], early_send.at[d, p, e], early_recv.at[d, p, slot],
            device_id=(ring_to[d] - core + e, sec), device_id_type=MESH)

    def early_wait(d, p, slot):
        pltpu.make_async_remote_copy(
            sendu.at[d, p, slot], recvu.at[d, p, slot], early_send.at[d, p, slot], early_recv.at[d, p, slot],
            device_id=(ring_to[d], sec), device_id_type=MESH).wait_recv()

    def early_terms(p):
        for d in range(2):
            if p == 0:
                g_copy(d, 0).wait()
            lo = d * half + p * PART
            early = jnp.dot(xet, gv[:seq, lo:lo + PART], preferred_element_type=F32).astype(BF16)
            for e in range(2):
                sendu[d, p, e] = early[e * rows:(e + 1) * rows]

    def early_start(p):
        for e in range(2):
            for d in range(2):
                early_copy(d, p, e).start()

    early_terms(0)
    lens[0] = jnp.full(lens.shape[1:], len_ref[0], F32)
    pl.semaphore_wait(barrier, len(peers))
    early_start(0)
    len_swap = pltpu.make_async_remote_copy(
        lens.at[0], lens.at[1], len_sem.at[0], len_sem.at[1], device_id=(partner, sec), device_id_type=MESH)
    len_swap.start()
    xb_swap(first).start()
    for h in range(2):
        g_swap(h, 1).start()

    def gram(acc, block, new=False):
        nt = (((1,), (1,)), ((), ()))
        left = lax.dot_general(block[:mid], block[:mid], nt, preferred_element_type=F32)
        right = lax.dot_general(block, block[mid:], nt, preferred_element_type=F32)
        if new:
            acc[:mid, :mid] = left
            acc[:, mid:] = right
        else:
            acc[:mid, :mid] += left
            acc[:, mid:] += right

    x_copy.wait()
    gram(gin, xv[...], True)
    for p in range(1, EARLY):
        early_terms(p)
        early_start(p)
    for h in range(2):
        g_copy(h, 1).wait()
        gram(gout, gv[:seq, h * half:(h + 1) * half], h == 0)

    row = lax.broadcasted_iota(jnp.int32, (seq, mid), 0)
    col = lax.broadcasted_iota(jnp.int32, (seq, mid), 1)
    n_live = len_ref[0]
    left_live = (row[:mid] < n_live) & (col[:mid] < n_live)
    left = jnp.where(left_live, gin[:mid, :mid] * gout[:mid, :mid], 0.0)
    twice = jnp.where(row < mid, 2.0, 1.0)
    right_live = (row < n_live) & (col + mid < n_live)
    right = jnp.where(right_live, gin[:, mid:] * gout[:, mid:] * twice, 0.0)
    cells = left + right[:mid] + right[mid:]
    norm = jnp.sum(jnp.sum(cells, axis=0, keepdims=True), axis=1, keepdims=True)
    row_tile[...] = jnp.broadcast_to(norm, row_tile.shape)

    def row_copy(j, frm):
        return pltpu.make_async_remote_copy(
            row_tile, rows_in.at[frm], row_send.at[j], row_recv.at[frm], device_id=(dp, in_row(j)), device_id_type=MESH)

    def col_copy(e, j, frm):
        return pltpu.make_async_remote_copy(
            col_tile, cols_in.at[e, frm], col_send.at[e, j], col_recv.at[e, frm],
            device_id=(partner if e else dp, in_col(j)), device_id_type=MESH)

    for j in range(1, side):
        row_copy(j, sec_x).start()
    rows_in[sec_x] = row_tile[...]

    token = lax.broadcasted_iota(jnp.int32, (seq, rows), 0).astype(F32)

    def turn(k):
        xb_swap(k).wait_recv()
        for e, block in enumerate((xv[:, x_cols(k, core)], xb[k])):
            block = jnp.where(token < lens[e, 0:1, :], block.astype(F32), 0.0)
            xt[k, :, e * seq:(e + 1) * seq] = block.T.astype(BF16)

    def scale(k):
        for e in range(2):
            factor = facs[e, 0:1, :]
            for j in range(seq // 128):
                cols = slice(e * seq + j * 128, e * seq + (j + 1) * 128)
                xt[k, :, cols] = (xt[k, :, cols].astype(F32) * factor).astype(BF16)

    for j in range(1, side):
        row_copy(j, lax.rem(sec_x + j, side)).wait_recv()
    col_tile[...] = jnp.sum(rows_in[...], axis=0)
    for j in range(side):
        col_copy(1, j, sec_y).start()
        if j:
            col_copy(0, j, sec_y).start()
    cols_in[0, sec_y] = col_tile[...]
    for k in (1, 2):
        xb_swap(owner(k)).start()
    for h in range(2):
        g_swap(h, 0).start()

    len_swap.wait_recv()
    turn(first)
    rest = [(lo, min(lo + width, half)) for lo in range(gone, half, width)]
    for d in range(2):
        g_swap(d, 1).wait_recv()
        for lo, hi in rest:
            for e in range(2):
                tokens = slice(e * seq, (e + 1) * seq)
                pre[d, e, :, lo - gone:hi - gone] = jnp.dot(
                    xt[first, :, tokens], gv[tokens, d * half + lo:d * half + hi], preferred_element_type=F32)

    for j in range(side):
        frm = lax.rem(sec_y + j, side)
        col_copy(1, j, frm).wait_recv()
        if j:
            col_copy(0, j, frm).wait_recv()
    for e in range(2):
        facs[e] = jnp.minimum(1.0, 1.0 / jnp.sqrt(jnp.sum(cols_in[e], axis=0) + 1e-06))

    def up_copy(d):
        return pltpu.make_async_remote_copy(
            facs, upfac.at[d], up_send.at[d], up_recv.at[d], device_id=(ring_to[d], sec), device_id_type=MESH)

    def ring_copy(d, i, part=0):
        block = pl.ds(0, half)
        if isinstance(i, int) and i == 0:
            block = pl.ds(gone, half - gone)
        elif isinstance(i, int) and i == steps - 1:
            block = pl.ds(half - width, width) if part else pl.ds(0, half - width)
        return pltpu.make_async_remote_copy(
            sendb.at[d, i, :, block], recvb.at[d, i, :, block], ring_send.at[d, i + part], ring_recv.at[d, i + part],
            device_id=(ring_to[d], sec), device_id_type=MESH)

    def term(k, h, s):
        return jnp.dot(xt[k], gv[:, pl.ds(pl.multiple_of(h * half + s * width, 128), width)], preferred_element_type=F32)

    def target(d, i):
        dist = n_chips // 2 - lax.div(i + 1, 2)
        return lax.rem(z + dist, n_chips) if d == 0 else lax.rem(z + n_chips - dist, n_chips)

    def cols(s):
        return slice(s * width, (s + 1) * width)

    def across(factor, n):
        return jnp.concatenate([factor] * (n // 128), axis=1)

    def step(i, add=True):
        for d in range(2):
            for s in range(PIECES):
                part = term(target(d, i), lax.rem(i + d, 2), s)
                if add:
                    if s == 0:
                        ring_copy(d, i - 2).wait_recv()
                    part += recvb[d, i - 2, :, cols(s)].astype(F32)
                sendb[d, i, :, cols(s)] = part.astype(BF16)
                if isinstance(i, int) and i == steps - 1 and s == PIECES - 2:
                    ring_copy(d, i).start()
            ring_copy(d, i, isinstance(i, int) and i == steps - 1).start()

    for d in range(2):
        for lo, hi in rest:
            own, other = (pre[d, e, :, lo - gone:hi - gone] * across(facs[e, 0:1], hi - lo) for e in range(2))
            sendb[d, 0, :, lo:hi] = (own + other).astype(BF16)
        ring_copy(d, 0).start()
    for d in range(2):
        up_copy(d).start()

    @pl.loop(3, n_chips)
    def _(k):
        xb_swap(owner(k)).start()

    @pl.loop(1, 3)
    def _(k):
        turn(owner(k))
        scale(owner(k))

    for h in range(2):
        g_swap(h, 0).wait_recv()
    step(1, add=False)

    @pl.loop(3, n_chips)
    def _(k):
        turn(owner(k))
        scale(owner(k))

    for d in range(2):
        up_copy(d).wait_recv()
        for p in range(EARLY):
            lo, hi = p * PART, (p + 1) * PART
            part = jnp.dot(xt[target(d, 2)], gv[:, d * half + lo:d * half + hi], preferred_element_type=F32)
            for e in range(2):
                early_wait(d, p, e)
                part += recvu[d, p, e].astype(F32) * across(upfac[d, e, 0:1], PART)
            sendb[d, 2, :, lo:hi] = part.astype(BF16)
        for lo, hi in rest:
            part = jnp.dot(xt[target(d, 2)], gv[:, d * half + lo:d * half + hi], preferred_element_type=F32)
            if lo == gone:
                ring_copy(d, 0).wait_recv()
            sendb[d, 2, :, lo:hi] = (part + recvb[d, 0, :, lo:hi].astype(F32)).astype(BF16)
        ring_copy(d, 2).start()

    @pl.loop(3, steps - 1)
    def _(i):
        step(i)

    step(steps - 1)

    for d in range(2):
        for s in range(PIECES):
            part = term(z, d, s)
            if s == 0:
                ring_copy(1 - d, steps - 2).wait_recv()
            fin[d * PIECES + s] = part + recvb[1 - d, steps - 2, :, cols(s)].astype(F32)

    for s in range(PIECES):
        for d in range(2):
            c = d * PIECES + s
            if s == 0 or s == PIECES - 1:
                ring_copy(d, steps - 1, int(s > 0)).wait_recv()
            done = (fin[c] + recvb[d, steps - 1, :, cols(s)].astype(F32)) * weight
            out_ref[:, cols(c)] = done.astype(out_ref.dtype)

    len_swap.wait_send()
    for d in range(2):
        up_copy(d).wait_send()
        for e in range(2):
            for p in range(EARLY):
                early_copy(d, p, e).wait_send()
            g_swap(d, e).wait_send()
        for i in range(steps):
            ring_copy(d, i).wait_send()
        ring_copy(d, steps - 1, 1).wait_send()
    for j in range(side):
        col_copy(1, j, sec_y).wait_send()
        if j:
            row_copy(j, sec_x).wait_send()
            col_copy(0, j, sec_y).wait_send()

    @pl.loop(0, n_chips)
    def _(k):
        xb_swap(k).wait_send()


def shards(layer_inputs, output_grads, lengths):
    n_dp, n_sec = lax.axis_size("dp"), lax.axis_size("section")
    inputs = layer_inputs[0, 0]
    grads = output_grads[0, 0]
    seq, din = inputs.shape
    dout = grads.shape[1]
    rows = din // n_dp
    n_chips = n_dp // 2
    steps = n_chips - 1
    half = dout // 2
    width = half // PIECES
    side = math.isqrt(n_sec)
    weight = math.sqrt(din * dout * n_sec / n_dp)
    dma = pltpu.SemaphoreType.DMA
    vmem = pltpu.VMEM
    out = pl.pallas_call(
        functools.partial(kernel, (n_chips, side, rows), weight),
        out_shape=jax.ShapeDtypeStruct((rows, dout), BF16),
        in_specs=[
            pl.BlockSpec(memory_space=pltpu.SMEM),
            pl.BlockSpec(memory_space=pl.ANY),
            pl.BlockSpec(memory_space=pl.ANY),
        ],
        out_specs=pl.BlockSpec(memory_space=pltpu.VMEM),
        scratch_shapes=dict(
            xe=vmem((seq, 2 * rows), BF16),
            xv=vmem((seq, din), BF16),
            xb=vmem((n_chips, seq, rows), BF16),
            gv=vmem((2 * seq, dout), BF16),
            xt=vmem((n_chips, rows, 2 * seq), BF16),
            sendb=vmem((2, steps, rows, half), BF16),
            recvb=vmem((2, steps, rows, half), BF16),
            sendu=vmem((2, EARLY, 2, rows, PART), BF16),
            recvu=vmem((2, EARLY, 2, rows, PART), BF16),
            pre=vmem((2, 2, rows, half - EARLY * PART), F32),
            fin=vmem((2 * PIECES, rows, width), F32),
            gin=vmem((seq, seq), F32),
            gout=vmem((seq, seq), F32),
            row_tile=vmem((8, 128), F32),
            col_tile=vmem((8, 128), F32),
            rows_in=vmem((side, 8, 128), F32),
            cols_in=vmem((2, side, 8, 128), F32),
            lens=vmem((2, 8, 128), F32),
            facs=vmem((2, 8, 128), F32),
            upfac=vmem((2, 2, 8, 128), F32),
            xe_sem=dma,
            xv_sem=dma,
            g_sem=dma((2, 2)),
            xb_send=dma((n_chips,)),
            xb_recv=dma((n_chips,)),
            g_send=dma((2, 2)),
            g_recv=dma((2, 2)),
            len_sem=dma((2,)),
            row_send=dma((side,)),
            row_recv=dma((side,)),
            col_send=dma((2, side)),
            col_recv=dma((2, side)),
            early_send=dma((2, EARLY, 2)),
            early_recv=dma((2, EARLY, 2)),
            up_send=dma((2,)),
            up_recv=dma((2,)),
            ring_send=dma((2, steps + 1)),
            ring_recv=dma((2, steps + 1)),
        ),
        compiler_params=pltpu.CompilerParams(
            collective_id=0, has_side_effects=True, vmem_limit_bytes=52 * 2**20
        ),
        cost_estimate=pl.CostEstimate(
            flops=2 * seq * din * dout + 2 * seq * seq * (din + dout), bytes_accessed=2 * seq * (din + dout),
            transcendentals=0,
        ),
    )(lengths, inputs, grads)
    return out[None]


def solution(mesh):
    placed = (P("section", "dp", None, None), P("section", "dp", None, None), P("dp"))
    return jax.shard_map(
        shards, mesh=mesh, in_specs=placed, out_specs=P("section", "dp", None), check_vma=False
    )
```

```python
import functools
import math

import jax
import jax.numpy as jnp
from jax import lax
from jax.experimental import pallas as pl
from jax.experimental.pallas import tpu as pltpu
from jax.sharding import PartitionSpec as P

F32 = jnp.float32
BF16 = jnp.bfloat16
MESH = pl.DeviceIdType.MESH
PIECES = 3
EARLY = ((0, 768), (768, 1152))


def kernel(dims, weight, len_ref, x_ref, g_ref, out_ref, xe, xv, xb, gv, xt, sendb, recvb, sendu, recvu, pre, fin, gin, gout,
           row_tile, col_tile, rows_in, cols_in, lens, facs, upfac, xe_sem, xv_sem, g_sem, xb_send, xb_recv, g_send, g_recv,
           len_sem, row_send, row_recv, col_send, col_recv, early_send, early_recv, up_send, up_recv, ring_send, ring_recv):
    n_chips, side, rows = dims
    seq = x_ref.shape[0]
    half = sendb.shape[3]
    width = half // PIECES
    gone = EARLY[-1][1]
    rest = ((gone, half - width), (half - width, half))
    mid = seq // 2
    steps = n_chips - 1
    dp = lax.axis_index("dp")
    sec = lax.axis_index("section")
    z = lax.div(dp, 2)
    core = lax.rem(dp, 2)
    partner = dp + 1 - 2 * core
    ahead = lax.rem(dp + 2, 2 * n_chips)
    behind = lax.rem(dp + 2 * n_chips - 2, 2 * n_chips)
    ring_to = (ahead, behind)
    sec_x = lax.div(sec, side)
    sec_y = lax.rem(sec, side)

    def in_row(j):
        return lax.rem(sec_x + j, side) * side + sec_y

    def in_col(j):
        return sec_x * side + lax.rem(sec_y + j, side)

    def owner(k):
        far = lax.div(k + 1, 2)
        turn = jnp.where(lax.rem(k, 2) == 1, n_chips - far, far)
        return lax.rem(z + n_chips // 2 + turn, n_chips)

    def x_cols(k, c):
        return pl.ds(pl.multiple_of((2 * k + c) * rows, 128), rows)

    def g_cols(h, part):
        return pl.ds(h * half + gone, half - gone) if part else pl.ds(h * half, gone)

    def g_copy(h, part):
        cols = g_cols(h, part)
        return pltpu.make_async_copy(g_ref.at[:, cols], gv.at[pl.ds(0, seq), cols], g_sem.at[h, part])

    def g_swap(h, part):
        cols = g_cols(h, part)
        return pltpu.make_async_remote_copy(
            g_ref.at[:, cols], gv.at[pl.ds(seq, seq), cols], g_send.at[h, part], g_recv.at[h, part],
            device_id=(partner, sec), device_id_type=MESH)

    def xb_swap(k):
        return pltpu.make_async_remote_copy(
            x_ref.at[:, x_cols(k, 1 - core)], xb.at[k], xb_send.at[k], xb_recv.at[k],
            device_id=(partner, sec), device_id_type=MESH)

    first = owner(0)
    xe_cols = pl.ds(pl.multiple_of(2 * first * rows, 128), 2 * rows)
    xe_copy = pltpu.make_async_copy(x_ref.at[:, xe_cols], xe, xe_sem)
    x_copy = pltpu.make_async_copy(x_ref, xv, xv_sem)
    xe_copy.start()
    for h in range(2):
        g_copy(h, 0).start()

    barrier = pltpu.get_barrier_semaphore()
    peers = [(peer + other, sec) for peer in ring_to for other in (0, partner - dp)]
    peers += [(dp, in_row(j)) for j in range(1, side)] + [(dp, in_col(j)) for j in range(1, side)]
    peers += [(partner, in_col(j)) for j in range(side)]
    for peer in peers:
        pl.semaphore_signal(barrier, inc=1, device_id=peer, device_id_type=MESH)
    x_copy.start()
    for h in range(2):
        g_copy(h, 1).start()

    xe_copy.wait()
    token = lax.broadcasted_iota(jnp.int32, xe.shape, 0)
    xet = jnp.where(token < len_ref[0], xe[...].astype(F32), 0.0).T.astype(BF16)

    def early_copy(d, p, e, slot):
        block = pl.ds(EARLY[p][0], EARLY[p][1] - EARLY[p][0])
        return pltpu.make_async_remote_copy(
            sendu.at[d, e, :, block], recvu.at[d, slot, :, block], early_send.at[d, p, e], early_recv.at[d, p, slot],
            device_id=(ring_to[d] - core + e, sec), device_id_type=MESH)

    def early_terms(p):
        for d in range(2):
            if p == 0:
                g_copy(d, 0).wait()
            lo, hi = EARLY[p]
            early = jnp.dot(xet, gv[:seq, d * half + lo:d * half + hi], preferred_element_type=F32).astype(BF16)
            for e in range(2):
                sendu[d, e, :, lo:hi] = early[e * rows:(e + 1) * rows]

    def early_start(p):
        for e in range(2):
            for d in range(2):
                early_copy(d, p, e, lax.rem(core + e, 2)).start()

    early_terms(0)
    lens[0] = jnp.full(lens.shape[1:], len_ref[0], F32)
    pl.semaphore_wait(barrier, len(peers))
    early_start(0)
    len_swap = pltpu.make_async_remote_copy(
        lens.at[0], lens.at[1], len_sem.at[0], len_sem.at[1], device_id=(partner, sec), device_id_type=MESH)
    len_swap.start()
    xb_swap(first).start()
    for h in range(2):
        g_swap(h, 1).start()

    def gram(acc, block, new=False):
        nt = (((1,), (1,)), ((), ()))
        top = lax.dot_general(block[:mid], block, nt, preferred_element_type=F32)
        low = lax.dot_general(block[mid:], block[mid:], nt, preferred_element_type=F32)
        if new:
            acc[:mid] = top
            acc[mid:, mid:] = low
        else:
            acc[:mid] += top
            acc[mid:, mid:] += low

    x_copy.wait()
    gram(gin, xv[...], True)
    for h in range(2):
        g_copy(h, 1).wait()
        gram(gout, gv[:seq, h * half:(h + 1) * half], h == 0)

    row = lax.broadcasted_iota(jnp.int32, (mid, seq), 0)
    col = lax.broadcasted_iota(jnp.int32, (mid, seq), 1)
    n_live = len_ref[0]
    twice = jnp.where(col >= mid, 2.0, 1.0)
    top = jnp.where((row < n_live) & (col < n_live), gin[:mid] * gout[:mid] * twice, 0.0)
    low_live = (row[:, mid:] + mid < n_live) & (col[:, mid:] < n_live)
    low = jnp.where(low_live, gin[mid:, mid:] * gout[mid:, mid:], 0.0)
    cells = top[:, :mid] + top[:, mid:] + low
    norm = jnp.sum(jnp.sum(cells, axis=0, keepdims=True), axis=1, keepdims=True)
    row_tile[...] = jnp.broadcast_to(norm, row_tile.shape)

    def row_copy(j, frm):
        return pltpu.make_async_remote_copy(
            row_tile, rows_in.at[frm], row_send.at[j], row_recv.at[frm], device_id=(dp, in_row(j)), device_id_type=MESH)

    def col_copy(e, j, frm):
        return pltpu.make_async_remote_copy(
            col_tile, cols_in.at[e, frm], col_send.at[e, j], col_recv.at[e, frm],
            device_id=(partner if e else dp, in_col(j)), device_id_type=MESH)

    for j in range(1, side):
        row_copy(j, sec_x).start()
    rows_in[sec_x] = row_tile[...]
    for p in range(1, len(EARLY)):
        early_terms(p)
        early_start(p)

    token = lax.broadcasted_iota(jnp.int32, (seq, rows), 0).astype(F32)

    def turn(k):
        xb_swap(k).wait_recv()
        for e, block in enumerate((xv[:, x_cols(k, core)], xb[k])):
            block = jnp.where(token < lens[e, 0:1, :], block.astype(F32), 0.0)
            xt[k, :, e * seq:(e + 1) * seq] = block.T.astype(BF16)

    def scale(k):
        for e in range(2):
            factor = facs[e, 0:1, :]
            for j in range(seq // 128):
                cols = slice(e * seq + j * 128, e * seq + (j + 1) * 128)
                xt[k, :, cols] = (xt[k, :, cols].astype(F32) * factor).astype(BF16)

    for j in range(1, side):
        row_copy(j, lax.rem(sec_x + j, side)).wait_recv()
    col_tile[...] = jnp.sum(rows_in[...], axis=0)
    for j in range(side):
        col_copy(1, j, sec_y).start()
        if j:
            col_copy(0, j, sec_y).start()
    cols_in[0, sec_y] = col_tile[...]
    for k in (1, 2):
        xb_swap(owner(k)).start()
    for h in range(2):
        g_swap(h, 0).start()

    len_swap.wait_recv()
    turn(first)
    lo, hi = rest[0]
    for d in range(2):
        g_swap(d, 1).wait_recv()
        for e in range(2):
            tokens = slice(e * seq, (e + 1) * seq)
            pre[d, e] = jnp.dot(
                xt[first, :, tokens], gv[tokens, d * half + lo:d * half + hi], preferred_element_type=F32)

    for j in range(side):
        frm = lax.rem(sec_y + j, side)
        col_copy(1, j, frm).wait_recv()
        if j:
            col_copy(0, j, frm).wait_recv()
    for e in range(2):
        facs[e] = jnp.minimum(1.0, 1.0 / jnp.sqrt(jnp.sum(cols_in[e], axis=0) + 1e-06))

    def up_copy(d):
        return pltpu.make_async_remote_copy(
            facs, upfac.at[d], up_send.at[d], up_recv.at[d], device_id=(ring_to[d], sec), device_id_type=MESH)

    def ring_copy(d, i, part=0):
        block = pl.ds(0, half)
        sem = i + part
        if isinstance(i, int) and i == 0:
            block = pl.ds(rest[part][0], rest[part][1] - rest[part][0])
            sem = part * (steps + 1)
        elif isinstance(i, int) and i == steps - 1:
            block = pl.ds(half - width, width) if part else pl.ds(0, half - width)
        return pltpu.make_async_remote_copy(
            sendb.at[d, i, :, block], recvb.at[d, i, :, block], ring_send.at[d, sem], ring_recv.at[d, sem],
            device_id=(ring_to[d], sec), device_id_type=MESH)

    def term(k, h, s):
        return jnp.dot(xt[k], gv[:, pl.ds(pl.multiple_of(h * half + s * width, 128), width)], preferred_element_type=F32)

    def target(d, i):
        dist = n_chips // 2 - lax.div(i + 1, 2)
        return lax.rem(z + dist, n_chips) if d == 0 else lax.rem(z + n_chips - dist, n_chips)

    def cols(s):
        return slice(s * width, (s + 1) * width)

    def across(factor, n):
        return jnp.concatenate([factor] * (n // 128), axis=1)

    def step(i, add=True):
        for d in range(2):
            for s in range(PIECES):
                part = term(target(d, i), lax.rem(i + d, 2), s)
                if add:
                    if s == 0:
                        ring_copy(d, i - 2).wait_recv()
                    part += recvb[d, i - 2, :, cols(s)].astype(F32)
                sendb[d, i, :, cols(s)] = part.astype(BF16)
                if isinstance(i, int) and i == steps - 1 and s == PIECES - 2:
                    ring_copy(d, i).start()
            ring_copy(d, i, isinstance(i, int) and i == steps - 1).start()

    lo, hi = rest[0]
    for d in range(2):
        own, other = (pre[d, e] * across(facs[e, 0:1], hi - lo) for e in range(2))
        sendb[d, 0, :, lo:hi] = (own + other).astype(BF16)
        ring_copy(d, 0).start()
    scale(first)
    lo, hi = rest[1]
    for d in range(2):
        part = jnp.dot(xt[first], gv[:, d * half + lo:d * half + hi], preferred_element_type=F32)
        sendb[d, 0, :, lo:hi] = part.astype(BF16)
        ring_copy(d, 0, 1).start()
    for d in range(2):
        up_copy(d).start()

    @pl.loop(3, n_chips)
    def _(k):
        xb_swap(owner(k)).start()

    @pl.loop(1, 3)
    def _(k):
        turn(owner(k))
        scale(owner(k))

    for h in range(2):
        g_swap(h, 0).wait_recv()
    step(1, add=False)

    @pl.loop(3, n_chips)
    def _(k):
        turn(owner(k))
        scale(owner(k))

    for d in range(2):
        up_copy(d).wait_recv()
        for p, (lo, hi) in enumerate(EARLY):
            part = jnp.dot(xt[target(d, 2)], gv[:, d * half + lo:d * half + hi], preferred_element_type=F32)
            for e in range(2):
                early_copy(d, p, e, e).wait_recv()
                part += recvu[d, e, :, lo:hi].astype(F32) * across(upfac[d, e, 0:1], hi - lo)
            sendb[d, 2, :, lo:hi] = part.astype(BF16)
        for p, (lo, hi) in enumerate(rest):
            part = jnp.dot(xt[target(d, 2)], gv[:, d * half + lo:d * half + hi], preferred_element_type=F32)
            ring_copy(d, 0, p).wait_recv()
            sendb[d, 2, :, lo:hi] = (part + recvb[d, 0, :, lo:hi].astype(F32)).astype(BF16)
        ring_copy(d, 2).start()

    @pl.loop(3, steps - 1)
    def _(i):
        step(i)

    step(steps - 1)

    for d in range(2):
        for s in range(PIECES):
            part = term(z, d, s)
            if s == 0:
                ring_copy(1 - d, steps - 2).wait_recv()
            fin[d * PIECES + s] = part + recvb[1 - d, steps - 2, :, cols(s)].astype(F32)

    for s in range(PIECES):
        for d in range(2):
            c = d * PIECES + s
            if s == 0 or s == PIECES - 1:
                ring_copy(d, steps - 1, int(s > 0)).wait_recv()
            done = (fin[c] + recvb[d, steps - 1, :, cols(s)].astype(F32)) * weight
            out_ref[:, cols(c)] = done.astype(out_ref.dtype)

    len_swap.wait_send()
    for d in range(2):
        up_copy(d).wait_send()
        for e in range(2):
            for p in range(len(EARLY)):
                early_copy(d, p, e, e).wait_send()
            g_swap(d, e).wait_send()
        for i in range(steps):
            ring_copy(d, i).wait_send()
        for i in (0, steps - 1):
            ring_copy(d, i, 1).wait_send()
    for j in range(side):
        col_copy(1, j, sec_y).wait_send()
        if j:
            row_copy(j, sec_x).wait_send()
            col_copy(0, j, sec_y).wait_send()

    @pl.loop(0, n_chips)
    def _(k):
        xb_swap(k).wait_send()


def shards(layer_inputs, output_grads, lengths):
    n_dp, n_sec = lax.axis_size("dp"), lax.axis_size("section")
    inputs = layer_inputs[0, 0]
    grads = output_grads[0, 0]
    seq, din = inputs.shape
    dout = grads.shape[1]
    rows = din // n_dp
    n_chips = n_dp // 2
    steps = n_chips - 1
    half = dout // 2
    width = half // PIECES
    side = math.isqrt(n_sec)
    gone = EARLY[-1][1]
    weight = math.sqrt(din * dout * n_sec / n_dp)
    dma = pltpu.SemaphoreType.DMA
    vmem = pltpu.VMEM
    out = pl.pallas_call(
        functools.partial(kernel, (n_chips, side, rows), weight),
        out_shape=jax.ShapeDtypeStruct((rows, dout), BF16),
        in_specs=[
            pl.BlockSpec(memory_space=pltpu.SMEM),
            pl.BlockSpec(memory_space=pl.ANY),
            pl.BlockSpec(memory_space=pl.ANY),
        ],
        out_specs=pl.BlockSpec(memory_space=pltpu.VMEM),
        scratch_shapes=dict(
            xe=vmem((seq, 2 * rows), BF16),
            xv=vmem((seq, din), BF16),
            xb=vmem((n_chips, seq, rows), BF16),
            gv=vmem((2 * seq, dout), BF16),
            xt=vmem((n_chips, rows, 2 * seq), BF16),
            sendb=vmem((2, steps, rows, half), BF16),
            recvb=vmem((2, steps, rows, half), BF16),
            sendu=vmem((2, 2, rows, gone), BF16),
            recvu=vmem((2, 2, rows, gone), BF16),
            pre=vmem((2, 2, rows, half - width - gone), F32),
            fin=vmem((2 * PIECES, rows, width), F32),
            gin=vmem((seq, seq), F32),
            gout=vmem((seq, seq), F32),
            row_tile=vmem((8, 128), F32),
            col_tile=vmem((8, 128), F32),
            rows_in=vmem((side, 8, 128), F32),
            cols_in=vmem((2, side, 8, 128), F32),
            lens=vmem((2, 8, 128), F32),
            facs=vmem((2, 8, 128), F32),
            upfac=vmem((2, 2, 8, 128), F32),
            xe_sem=dma,
            xv_sem=dma,
            g_sem=dma((2, 2)),
            xb_send=dma((n_chips,)),
            xb_recv=dma((n_chips,)),
            g_send=dma((2, 2)),
            g_recv=dma((2, 2)),
            len_sem=dma((2,)),
            row_send=dma((side,)),
            row_recv=dma((side,)),
            col_send=dma((2, side)),
            col_recv=dma((2, side)),
            early_send=dma((2, len(EARLY), 2)),
            early_recv=dma((2, len(EARLY), 2)),
            up_send=dma((2,)),
            up_recv=dma((2,)),
            ring_send=dma((2, steps + 2)),
            ring_recv=dma((2, steps + 2)),
        ),
        compiler_params=pltpu.CompilerParams(
            collective_id=0, has_side_effects=True, vmem_limit_bytes=52 * 2**20
        ),
        cost_estimate=pl.CostEstimate(
            flops=2 * seq * din * dout + 2 * seq * seq * (din + dout), bytes_accessed=2 * seq * (din + dout),
            transcendentals=0,
        ),
    )(lengths, inputs, grads)
    return out[None]


def solution(mesh):
    placed = (P("section", "dp", None, None), P("section", "dp", None, None), P("dp"))
    return jax.shard_map(
        shards, mesh=mesh, in_specs=placed, out_specs=P("section", "dp", None), check_vma=False
    )
```

```python
import functools
import math

import jax
import jax.numpy as jnp
from jax import lax
from jax.experimental import pallas as pl
from jax.experimental.pallas import tpu as pltpu
from jax.sharding import PartitionSpec as P

F32 = jnp.float32
BF16 = jnp.bfloat16
MESH = pl.DeviceIdType.MESH
PIECES = 3
EARLY = ((0, 512), (512, 1152))


def kernel(dims, weight, len_ref, x_ref, g_ref, out_ref, xe, xv, xb, gv, xt, sendb, recvb, sendu, recvu, pre, fin, gin, gout,
           row_tile, col_tile, rows_in, cols_in, lens, facs, upfac, xe_sem, xv_sem, g_sem, xb_send, xb_recv, g_send, g_recv,
           len_sem, row_send, row_recv, col_send, col_recv, early_send, early_recv, up_send, up_recv, ring_send, ring_recv):
    n_chips, side, rows = dims
    seq = x_ref.shape[0]
    half = sendb.shape[3]
    width = half // PIECES
    gone = EARLY[-1][1]
    rest = ((gone, half - width), (half - width, half))
    mid = seq // 2
    steps = n_chips - 1
    dp = lax.axis_index("dp")
    sec = lax.axis_index("section")
    z = lax.div(dp, 2)
    core = lax.rem(dp, 2)
    partner = dp + 1 - 2 * core
    ahead = lax.rem(dp + 2, 2 * n_chips)
    behind = lax.rem(dp + 2 * n_chips - 2, 2 * n_chips)
    ring_to = (ahead, behind)
    sec_x = lax.div(sec, side)
    sec_y = lax.rem(sec, side)

    def in_row(j):
        return lax.rem(sec_x + j, side) * side + sec_y

    def in_col(j):
        return sec_x * side + lax.rem(sec_y + j, side)

    def owner(k):
        far = lax.div(k + 1, 2)
        turn = jnp.where(lax.rem(k, 2) == 1, n_chips - far, far)
        return lax.rem(z + n_chips // 2 + turn, n_chips)

    def x_cols(k, c):
        return pl.ds(pl.multiple_of((2 * k + c) * rows, 128), rows)

    def g_cols(h, part):
        return pl.ds(h * half + gone, half - gone) if part else pl.ds(h * half, gone)

    def g_copy(h, part):
        cols = g_cols(h, part)
        return pltpu.make_async_copy(g_ref.at[:, cols], gv.at[pl.ds(0, seq), cols], g_sem.at[h, part])

    def g_swap(h, part):
        cols = g_cols(h, part)
        return pltpu.make_async_remote_copy(
            g_ref.at[:, cols], gv.at[pl.ds(seq, seq), cols], g_send.at[h, part], g_recv.at[h, part],
            device_id=(partner, sec), device_id_type=MESH)

    def xb_swap(k):
        return pltpu.make_async_remote_copy(
            x_ref.at[:, x_cols(k, 1 - core)], xb.at[k], xb_send.at[k], xb_recv.at[k],
            device_id=(partner, sec), device_id_type=MESH)

    first = owner(0)
    xe_cols = pl.ds(pl.multiple_of(2 * first * rows, 128), 2 * rows)
    xe_copy = pltpu.make_async_copy(x_ref.at[:, xe_cols], xe, xe_sem)
    x_copy = pltpu.make_async_copy(x_ref, xv, xv_sem)
    xe_copy.start()
    for h in range(2):
        g_copy(h, 0).start()

    barrier = pltpu.get_barrier_semaphore()
    peers = [(peer + other, sec) for peer in ring_to for other in (0, partner - dp)]
    peers += [(dp, in_row(j)) for j in range(1, side)] + [(dp, in_col(j)) for j in range(1, side)]
    peers += [(partner, in_col(j)) for j in range(side)]
    for peer in peers:
        pl.semaphore_signal(barrier, inc=1, device_id=peer, device_id_type=MESH)
    x_copy.start()
    for h in range(2):
        g_copy(h, 1).start()

    xe_copy.wait()
    token = lax.broadcasted_iota(jnp.int32, xe.shape, 0)
    xet = jnp.where(token < len_ref[0], xe[...].astype(F32), 0.0).T.astype(BF16)

    def early_copy(d, p, e, slot):
        block = pl.ds(EARLY[p][0], EARLY[p][1] - EARLY[p][0])
        return pltpu.make_async_remote_copy(
            sendu.at[d, e, :, block], recvu.at[d, slot, :, block], early_send.at[d, p, e], early_recv.at[d, p, slot],
            device_id=(ring_to[d] - core + e, sec), device_id_type=MESH)

    def early_terms(p):
        for d in range(2):
            if p == 0:
                g_copy(d, 0).wait()
            lo, hi = EARLY[p]
            early = jnp.dot(xet, gv[:seq, d * half + lo:d * half + hi], preferred_element_type=F32).astype(BF16)
            for e in range(2):
                sendu[d, e, :, lo:hi] = early[e * rows:(e + 1) * rows]

    def early_start(p):
        for e in range(2):
            for d in range(2):
                early_copy(d, p, e, lax.rem(core + e, 2)).start()

    early_terms(0)
    lens[0] = jnp.full(lens.shape[1:], len_ref[0], F32)
    pl.semaphore_wait(barrier, len(peers))
    early_start(0)
    len_swap = pltpu.make_async_remote_copy(
        lens.at[0], lens.at[1], len_sem.at[0], len_sem.at[1], device_id=(partner, sec), device_id_type=MESH)
    len_swap.start()
    xb_swap(first).start()
    for h in range(2):
        g_swap(h, 1).start()

    def gram(acc, block, new=False):
        nt = (((1,), (1,)), ((), ()))
        left = lax.dot_general(block[:mid], block[:mid], nt, preferred_element_type=F32)
        right = lax.dot_general(block, block[mid:], nt, preferred_element_type=F32)
        if new:
            acc[:mid, :mid] = left
            acc[:, mid:] = right
        else:
            acc[:mid, :mid] += left
            acc[:, mid:] += right

    x_copy.wait()
    gram(gin, xv[...], True)
    for p in range(1, len(EARLY)):
        early_terms(p)
        early_start(p)
    for h in range(2):
        g_copy(h, 1).wait()
        gram(gout, gv[:seq, h * half:(h + 1) * half], h == 0)

    row = lax.broadcasted_iota(jnp.int32, (seq, mid), 0)
    col = lax.broadcasted_iota(jnp.int32, (seq, mid), 1)
    n_live = len_ref[0]
    left_live = (row[:mid] < n_live) & (col[:mid] < n_live)
    left = jnp.where(left_live, gin[:mid, :mid] * gout[:mid, :mid], 0.0)
    twice = jnp.where(row < mid, 2.0, 1.0)
    right_live = (row < n_live) & (col + mid < n_live)
    right = jnp.where(right_live, gin[:, mid:] * gout[:, mid:] * twice, 0.0)
    cells = left + right[:mid] + right[mid:]
    norm = jnp.sum(jnp.sum(cells, axis=0, keepdims=True), axis=1, keepdims=True)
    row_tile[...] = jnp.broadcast_to(norm, row_tile.shape)

    def row_copy(j, frm):
        return pltpu.make_async_remote_copy(
            row_tile, rows_in.at[frm], row_send.at[j], row_recv.at[frm], device_id=(dp, in_row(j)), device_id_type=MESH)

    def col_copy(e, j, frm):
        return pltpu.make_async_remote_copy(
            col_tile, cols_in.at[e, frm], col_send.at[e, j], col_recv.at[e, frm],
            device_id=(partner if e else dp, in_col(j)), device_id_type=MESH)

    for j in range(1, side):
        row_copy(j, sec_x).start()
    rows_in[sec_x] = row_tile[...]

    token = lax.broadcasted_iota(jnp.int32, (seq, rows), 0).astype(F32)

    def turn(k):
        xb_swap(k).wait_recv()
        for e, block in enumerate((xv[:, x_cols(k, core)], xb[k])):
            block = jnp.where(token < lens[e, 0:1, :], block.astype(F32), 0.0)
            xt[k, :, e * seq:(e + 1) * seq] = block.T.astype(BF16)

    def scale(k):
        for e in range(2):
            factor = facs[e, 0:1, :]
            for j in range(seq // 128):
                cols = slice(e * seq + j * 128, e * seq + (j + 1) * 128)
                xt[k, :, cols] = (xt[k, :, cols].astype(F32) * factor).astype(BF16)

    for j in range(1, side):
        row_copy(j, lax.rem(sec_x + j, side)).wait_recv()
    col_tile[...] = jnp.sum(rows_in[...], axis=0)
    for j in range(side):
        col_copy(1, j, sec_y).start()
        if j:
            col_copy(0, j, sec_y).start()
    cols_in[0, sec_y] = col_tile[...]
    for k in (1, 2):
        xb_swap(owner(k)).start()
    for h in range(2):
        g_swap(h, 0).start()

    len_swap.wait_recv()
    turn(first)
    lo, hi = rest[0]
    for d in range(2):
        g_swap(d, 1).wait_recv()
        for e in range(2):
            tokens = slice(e * seq, (e + 1) * seq)
            pre[d, e] = jnp.dot(
                xt[first, :, tokens], gv[tokens, d * half + lo:d * half + hi], preferred_element_type=F32)

    for j in range(side):
        frm = lax.rem(sec_y + j, side)
        col_copy(1, j, frm).wait_recv()
        if j:
            col_copy(0, j, frm).wait_recv()
    for e in range(2):
        facs[e] = jnp.minimum(1.0, 1.0 / jnp.sqrt(jnp.sum(cols_in[e], axis=0) + 1e-06))

    def up_copy(d):
        return pltpu.make_async_remote_copy(
            facs, upfac.at[d], up_send.at[d], up_recv.at[d], device_id=(ring_to[d], sec), device_id_type=MESH)

    def ring_copy(d, i, part=0):
        block = pl.ds(0, half)
        sem = i + part
        if isinstance(i, int) and i == 0:
            block = pl.ds(rest[part][0], rest[part][1] - rest[part][0])
            sem = part * (steps + 1)
        elif isinstance(i, int) and i == steps - 1:
            block = pl.ds(half - width, width) if part else pl.ds(0, half - width)
        return pltpu.make_async_remote_copy(
            sendb.at[d, i, :, block], recvb.at[d, i, :, block], ring_send.at[d, sem], ring_recv.at[d, sem],
            device_id=(ring_to[d], sec), device_id_type=MESH)

    def term(k, h, s):
        return jnp.dot(xt[k], gv[:, pl.ds(pl.multiple_of(h * half + s * width, 128), width)], preferred_element_type=F32)

    def target(d, i):
        dist = n_chips // 2 - lax.div(i + 1, 2)
        return lax.rem(z + dist, n_chips) if d == 0 else lax.rem(z + n_chips - dist, n_chips)

    def cols(s):
        return slice(s * width, (s + 1) * width)

    def across(factor, n):
        return jnp.concatenate([factor] * (n // 128), axis=1)

    def step(i, add=True):
        for d in range(2):
            for s in range(PIECES):
                part = term(target(d, i), lax.rem(i + d, 2), s)
                if add:
                    if s == 0:
                        ring_copy(d, i - 2).wait_recv()
                    part += recvb[d, i - 2, :, cols(s)].astype(F32)
                sendb[d, i, :, cols(s)] = part.astype(BF16)
                if isinstance(i, int) and i == steps - 1 and s == PIECES - 2:
                    ring_copy(d, i).start()
            ring_copy(d, i, isinstance(i, int) and i == steps - 1).start()

    lo, hi = rest[0]
    for d in range(2):
        own, other = (pre[d, e] * across(facs[e, 0:1], hi - lo) for e in range(2))
        sendb[d, 0, :, lo:hi] = (own + other).astype(BF16)
        ring_copy(d, 0).start()
    scale(first)
    lo, hi = rest[1]
    for d in range(2):
        part = jnp.dot(xt[first], gv[:, d * half + lo:d * half + hi], preferred_element_type=F32)
        sendb[d, 0, :, lo:hi] = part.astype(BF16)
        ring_copy(d, 0, 1).start()
    for d in range(2):
        up_copy(d).start()

    @pl.loop(3, n_chips)
    def _(k):
        xb_swap(owner(k)).start()

    @pl.loop(1, 3)
    def _(k):
        turn(owner(k))
        scale(owner(k))

    for h in range(2):
        g_swap(h, 0).wait_recv()
    step(1, add=False)

    @pl.loop(3, n_chips)
    def _(k):
        turn(owner(k))
        scale(owner(k))

    for d in range(2):
        up_copy(d).wait_recv()
        for p, (lo, hi) in enumerate(EARLY):
            part = jnp.dot(xt[target(d, 2)], gv[:, d * half + lo:d * half + hi], preferred_element_type=F32)
            for e in range(2):
                early_copy(d, p, e, e).wait_recv()
                part += recvu[d, e, :, lo:hi].astype(F32) * across(upfac[d, e, 0:1], hi - lo)
            sendb[d, 2, :, lo:hi] = part.astype(BF16)
        for p, (lo, hi) in enumerate(rest):
            part = jnp.dot(xt[target(d, 2)], gv[:, d * half + lo:d * half + hi], preferred_element_type=F32)
            ring_copy(d, 0, p).wait_recv()
            sendb[d, 2, :, lo:hi] = (part + recvb[d, 0, :, lo:hi].astype(F32)).astype(BF16)
        ring_copy(d, 2).start()

    @pl.loop(3, steps - 1)
    def _(i):
        step(i)

    step(steps - 1)

    for d in range(2):
        for s in range(PIECES):
            part = term(z, d, s)
            if s == 0:
                ring_copy(1 - d, steps - 2).wait_recv()
            fin[d * PIECES + s] = part + recvb[1 - d, steps - 2, :, cols(s)].astype(F32)

    for s in range(PIECES):
        for d in range(2):
            c = d * PIECES + s
            if s == 0 or s == PIECES - 1:
                ring_copy(d, steps - 1, int(s > 0)).wait_recv()
            done = (fin[c] + recvb[d, steps - 1, :, cols(s)].astype(F32)) * weight
            out_ref[:, cols(c)] = done.astype(out_ref.dtype)

    len_swap.wait_send()
    for d in range(2):
        up_copy(d).wait_send()
        for e in range(2):
            for p in range(len(EARLY)):
                early_copy(d, p, e, e).wait_send()
            g_swap(d, e).wait_send()
        for i in range(steps):
            ring_copy(d, i).wait_send()
        for i in (0, steps - 1):
            ring_copy(d, i, 1).wait_send()
    for j in range(side):
        col_copy(1, j, sec_y).wait_send()
        if j:
            row_copy(j, sec_x).wait_send()
            col_copy(0, j, sec_y).wait_send()

    @pl.loop(0, n_chips)
    def _(k):
        xb_swap(k).wait_send()


def shards(layer_inputs, output_grads, lengths):
    n_dp, n_sec = lax.axis_size("dp"), lax.axis_size("section")
    inputs = layer_inputs[0, 0]
    grads = output_grads[0, 0]
    seq, din = inputs.shape
    dout = grads.shape[1]
    rows = din // n_dp
    n_chips = n_dp // 2
    steps = n_chips - 1
    half = dout // 2
    width = half // PIECES
    side = math.isqrt(n_sec)
    gone = EARLY[-1][1]
    weight = math.sqrt(din * dout * n_sec / n_dp)
    dma = pltpu.SemaphoreType.DMA
    vmem = pltpu.VMEM
    out = pl.pallas_call(
        functools.partial(kernel, (n_chips, side, rows), weight),
        out_shape=jax.ShapeDtypeStruct((rows, dout), BF16),
        in_specs=[
            pl.BlockSpec(memory_space=pltpu.SMEM),
            pl.BlockSpec(memory_space=pl.ANY),
            pl.BlockSpec(memory_space=pl.ANY),
        ],
        out_specs=pl.BlockSpec(memory_space=pltpu.VMEM),
        scratch_shapes=dict(
            xe=vmem((seq, 2 * rows), BF16),
            xv=vmem((seq, din), BF16),
            xb=vmem((n_chips, seq, rows), BF16),
            gv=vmem((2 * seq, dout), BF16),
            xt=vmem((n_chips, rows, 2 * seq), BF16),
            sendb=vmem((2, steps, rows, half), BF16),
            recvb=vmem((2, steps, rows, half), BF16),
            sendu=vmem((2, 2, rows, gone), BF16),
            recvu=vmem((2, 2, rows, gone), BF16),
            pre=vmem((2, 2, rows, half - width - gone), F32),
            fin=vmem((2 * PIECES, rows, width), F32),
            gin=vmem((seq, seq), F32),
            gout=vmem((seq, seq), F32),
            row_tile=vmem((8, 128), F32),
            col_tile=vmem((8, 128), F32),
            rows_in=vmem((side, 8, 128), F32),
            cols_in=vmem((2, side, 8, 128), F32),
            lens=vmem((2, 8, 128), F32),
            facs=vmem((2, 8, 128), F32),
            upfac=vmem((2, 2, 8, 128), F32),
            xe_sem=dma,
            xv_sem=dma,
            g_sem=dma((2, 2)),
            xb_send=dma((n_chips,)),
            xb_recv=dma((n_chips,)),
            g_send=dma((2, 2)),
            g_recv=dma((2, 2)),
            len_sem=dma((2,)),
            row_send=dma((side,)),
            row_recv=dma((side,)),
            col_send=dma((2, side)),
            col_recv=dma((2, side)),
            early_send=dma((2, len(EARLY), 2)),
            early_recv=dma((2, len(EARLY), 2)),
            up_send=dma((2,)),
            up_recv=dma((2,)),
            ring_send=dma((2, steps + 2)),
            ring_recv=dma((2, steps + 2)),
        ),
        compiler_params=pltpu.CompilerParams(
            collective_id=0, has_side_effects=True, vmem_limit_bytes=52 * 2**20
        ),
        cost_estimate=pl.CostEstimate(
            flops=2 * seq * din * dout + 2 * seq * seq * (din + dout), bytes_accessed=2 * seq * (din + dout),
            transcendentals=0,
        ),
    )(lengths, inputs, grads)
    return out[None]


def solution(mesh):
    placed = (P("section", "dp", None, None), P("section", "dp", None, None), P("dp"))
    return jax.shard_map(
        shards, mesh=mesh, in_specs=placed, out_specs=P("section", "dp", None), check_vma=False
    )
```

```python
import functools
import math

import jax
import jax.numpy as jnp
from jax import lax
from jax.experimental import pallas as pl
from jax.experimental.pallas import tpu as pltpu
from jax.sharding import PartitionSpec as P

F32 = jnp.float32
BF16 = jnp.bfloat16
MESH = pl.DeviceIdType.MESH
PIECES = 3
EARLY = ((0, 512), (512, 1152))


def kernel(dims, weight, len_ref, x_ref, g_ref, out_ref, xe, xv, xb, gv, xt, sendb, recvb, sendu, recvu, pre, fin, gin, gout,
           row_tile, col_tile, rows_in, cols_in, lens, facs, upfac, xe_sem, xv_sem, g_sem, xb_send, xb_recv, g_send, g_recv,
           len_sem, row_send, row_recv, col_send, col_recv, early_send, early_recv, up_send, up_recv, ring_send, ring_recv):
    n_chips, side, rows = dims
    seq = x_ref.shape[0]
    half = sendb.shape[3]
    width = half // PIECES
    gone = EARLY[-1][1]
    rest = ((gone, half - width), (half - width, half))
    mid = seq // 2
    steps = n_chips - 1
    dp = lax.axis_index("dp")
    sec = lax.axis_index("section")
    z = lax.div(dp, 2)
    core = lax.rem(dp, 2)
    partner = dp + 1 - 2 * core
    ahead = lax.rem(dp + 2, 2 * n_chips)
    behind = lax.rem(dp + 2 * n_chips - 2, 2 * n_chips)
    ring_to = (ahead, behind)
    sec_x = lax.div(sec, side)
    sec_y = lax.rem(sec, side)

    def in_row(j):
        return lax.rem(sec_x + j, side) * side + sec_y

    def in_col(j):
        return sec_x * side + lax.rem(sec_y + j, side)

    def owner(k):
        far = lax.div(k + 1, 2)
        turn = jnp.where(lax.rem(k, 2) == 1, n_chips - far, far)
        return lax.rem(z + n_chips // 2 + turn, n_chips)

    def x_cols(k, c):
        return pl.ds(pl.multiple_of((2 * k + c) * rows, 128), rows)

    def g_cols(h, part, cut):
        return pl.ds(h * half + cut, half - cut) if part else pl.ds(h * half, cut)

    def g_copy(h, part):
        cols = g_cols(h, part, EARLY[0][1])
        return pltpu.make_async_copy(g_ref.at[:, cols], gv.at[pl.ds(0, seq), cols], g_sem.at[h, part])

    def g_swap(h, part):
        cols = g_cols(h, part, gone)
        return pltpu.make_async_remote_copy(
            g_ref.at[:, cols], gv.at[pl.ds(seq, seq), cols], g_send.at[h, part], g_recv.at[h, part],
            device_id=(partner, sec), device_id_type=MESH)

    def xb_swap(k):
        return pltpu.make_async_remote_copy(
            x_ref.at[:, x_cols(k, 1 - core)], xb.at[k], xb_send.at[k], xb_recv.at[k],
            device_id=(partner, sec), device_id_type=MESH)

    first = owner(0)
    xe_cols = pl.ds(pl.multiple_of(2 * first * rows, 128), 2 * rows)
    xe_copy = pltpu.make_async_copy(x_ref.at[:, xe_cols], xe, xe_sem)
    x_copy = pltpu.make_async_copy(x_ref, xv, xv_sem)
    xe_copy.start()
    for h in range(2):
        g_copy(h, 0).start()

    barrier = pltpu.get_barrier_semaphore()
    peers = [(peer + other, sec) for peer in ring_to for other in (0, partner - dp)]
    peers += [(dp, in_row(j)) for j in range(1, side)] + [(dp, in_col(j)) for j in range(1, side)]
    peers += [(partner, in_col(j)) for j in range(side)]
    for peer in peers:
        pl.semaphore_signal(barrier, inc=1, device_id=peer, device_id_type=MESH)
    x_copy.start()
    for h in range(2):
        g_copy(h, 1).start()

    xe_copy.wait()
    token = lax.broadcasted_iota(jnp.int32, xe.shape, 0)
    xet = jnp.where(token < len_ref[0], xe[...].astype(F32), 0.0).T.astype(BF16)

    def early_copy(d, p, e, slot):
        block = pl.ds(EARLY[p][0], EARLY[p][1] - EARLY[p][0])
        return pltpu.make_async_remote_copy(
            sendu.at[d, e, :, block], recvu.at[d, slot, :, block], early_send.at[d, p, e], early_recv.at[d, p, slot],
            device_id=(ring_to[d] - core + e, sec), device_id_type=MESH)

    def early_terms(p):
        for d in range(2):
            if p < 2:
                g_copy(d, p).wait()
            lo, hi = EARLY[p]
            early = jnp.dot(xet, gv[:seq, d * half + lo:d * half + hi], preferred_element_type=F32).astype(BF16)
            for e in range(2):
                sendu[d, e, :, lo:hi] = early[e * rows:(e + 1) * rows]

    def early_start(p):
        for e in range(2):
            for d in range(2):
                early_copy(d, p, e, lax.rem(core + e, 2)).start()

    early_terms(0)
    lens[0] = jnp.full(lens.shape[1:], len_ref[0], F32)
    pl.semaphore_wait(barrier, len(peers))
    early_start(0)
    len_swap = pltpu.make_async_remote_copy(
        lens.at[0], lens.at[1], len_sem.at[0], len_sem.at[1], device_id=(partner, sec), device_id_type=MESH)

    def gram(acc, block, new=False):
        nt = (((1,), (1,)), ((), ()))
        left = lax.dot_general(block[:mid], block[:mid], nt, preferred_element_type=F32)
        right = lax.dot_general(block, block[mid:], nt, preferred_element_type=F32)
        if new:
            acc[:mid, :mid] = left
            acc[:, mid:] = right
        else:
            acc[:mid, :mid] += left
            acc[:, mid:] += right

    x_copy.wait()
    gram(gin, xv[...], True)
    len_swap.start()
    xb_swap(first).start()
    for h in range(2):
        g_swap(h, 1).start()
    for p in range(1, len(EARLY)):
        early_terms(p)
        early_start(p)
    for h in range(2):
        gram(gout, gv[:seq, h * half:(h + 1) * half], h == 0)

    row = lax.broadcasted_iota(jnp.int32, (seq, mid), 0)
    col = lax.broadcasted_iota(jnp.int32, (seq, mid), 1)
    n_live = len_ref[0]
    left_live = (row[:mid] < n_live) & (col[:mid] < n_live)
    left = jnp.where(left_live, gin[:mid, :mid] * gout[:mid, :mid], 0.0)
    twice = jnp.where(row < mid, 2.0, 1.0)
    right_live = (row < n_live) & (col + mid < n_live)
    right = jnp.where(right_live, gin[:, mid:] * gout[:, mid:] * twice, 0.0)
    cells = left + right[:mid] + right[mid:]
    norm = jnp.sum(jnp.sum(cells, axis=0, keepdims=True), axis=1, keepdims=True)
    row_tile[...] = jnp.broadcast_to(norm, row_tile.shape)

    def row_copy(j, frm):
        return pltpu.make_async_remote_copy(
            row_tile, rows_in.at[frm], row_send.at[j], row_recv.at[frm], device_id=(dp, in_row(j)), device_id_type=MESH)

    def col_copy(e, j, frm):
        return pltpu.make_async_remote_copy(
            col_tile, cols_in.at[e, frm], col_send.at[e, j], col_recv.at[e, frm],
            device_id=(partner if e else dp, in_col(j)), device_id_type=MESH)

    for j in range(1, side):
        row_copy(j, sec_x).start()
    rows_in[sec_x] = row_tile[...]

    token = lax.broadcasted_iota(jnp.int32, (seq, rows), 0).astype(F32)

    def turn(k):
        xb_swap(k).wait_recv()
        for e, block in enumerate((xv[:, x_cols(k, core)], xb[k])):
            block = jnp.where(token < lens[e, 0:1, :], block.astype(F32), 0.0)
            xt[k, :, e * seq:(e + 1) * seq] = block.T.astype(BF16)

    def scale(k):
        for e in range(2):
            factor = facs[e, 0:1, :]
            for j in range(seq // 128):
                cols = slice(e * seq + j * 128, e * seq + (j + 1) * 128)
                xt[k, :, cols] = (xt[k, :, cols].astype(F32) * factor).astype(BF16)

    for j in range(1, side):
        row_copy(j, lax.rem(sec_x + j, side)).wait_recv()
    col_tile[...] = jnp.sum(rows_in[...], axis=0)
    for j in range(side):
        col_copy(1, j, sec_y).start()
        if j:
            col_copy(0, j, sec_y).start()
    cols_in[0, sec_y] = col_tile[...]
    for k in (1, 2):
        xb_swap(owner(k)).start()
    for h in range(2):
        g_swap(h, 0).start()

    len_swap.wait_recv()
    turn(first)
    lo, hi = rest[0]
    for d in range(2):
        g_swap(d, 1).wait_recv()
        for e in range(2):
            tokens = slice(e * seq, (e + 1) * seq)
            pre[d, e] = jnp.dot(
                xt[first, :, tokens], gv[tokens, d * half + lo:d * half + hi], preferred_element_type=F32)

    for j in range(side):
        frm = lax.rem(sec_y + j, side)
        col_copy(1, j, frm).wait_recv()
        if j:
            col_copy(0, j, frm).wait_recv()
    for e in range(2):
        facs[e] = jnp.minimum(1.0, 1.0 / jnp.sqrt(jnp.sum(cols_in[e], axis=0) + 1e-06))

    def up_copy(d):
        return pltpu.make_async_remote_copy(
            facs, upfac.at[d], up_send.at[d], up_recv.at[d], device_id=(ring_to[d], sec), device_id_type=MESH)

    def ring_copy(d, i, part=0):
        block = pl.ds(0, half)
        sem = i + part
        if isinstance(i, int) and i == 0:
            block = pl.ds(rest[part][0], rest[part][1] - rest[part][0])
            sem = part * (steps + 1)
        elif isinstance(i, int) and i == steps - 1:
            block = pl.ds(half - width, width) if part else pl.ds(0, half - width)
        return pltpu.make_async_remote_copy(
            sendb.at[d, i, :, block], recvb.at[d, i, :, block], ring_send.at[d, sem], ring_recv.at[d, sem],
            device_id=(ring_to[d], sec), device_id_type=MESH)

    def term(k, h, s):
        return jnp.dot(xt[k], gv[:, pl.ds(pl.multiple_of(h * half + s * width, 128), width)], preferred_element_type=F32)

    def target(d, i):
        dist = n_chips // 2 - lax.div(i + 1, 2)
        return lax.rem(z + dist, n_chips) if d == 0 else lax.rem(z + n_chips - dist, n_chips)

    def cols(s):
        return slice(s * width, (s + 1) * width)

    def across(factor, n):
        return jnp.concatenate([factor] * (n // 128), axis=1)

    def step(i, add=True):
        for d in range(2):
            for s in range(PIECES):
                part = term(target(d, i), lax.rem(i + d, 2), s)
                if add:
                    if s == 0:
                        ring_copy(d, i - 2).wait_recv()
                    part += recvb[d, i - 2, :, cols(s)].astype(F32)
                sendb[d, i, :, cols(s)] = part.astype(BF16)
                if isinstance(i, int) and i == steps - 1 and s == PIECES - 2:
                    ring_copy(d, i).start()
            ring_copy(d, i, isinstance(i, int) and i == steps - 1).start()

    lo, hi = rest[0]
    for d in range(2):
        own, other = (pre[d, e] * across(facs[e, 0:1], hi - lo) for e in range(2))
        sendb[d, 0, :, lo:hi] = (own + other).astype(BF16)
        ring_copy(d, 0).start()
    scale(first)
    lo, hi = rest[1]
    for d in range(2):
        part = jnp.dot(xt[first], gv[:, d * half + lo:d * half + hi], preferred_element_type=F32)
        sendb[d, 0, :, lo:hi] = part.astype(BF16)
        ring_copy(d, 0, 1).start()
    for d in range(2):
        up_copy(d).start()

    @pl.loop(3, n_chips)
    def _(k):
        xb_swap(owner(k)).start()

    @pl.loop(1, 3)
    def _(k):
        turn(owner(k))
        scale(owner(k))

    for h in range(2):
        g_swap(h, 0).wait_recv()
    step(1, add=False)

    @pl.loop(3, n_chips)
    def _(k):
        turn(owner(k))
        scale(owner(k))

    for d in range(2):
        up_copy(d).wait_recv()
        for p, (lo, hi) in enumerate(EARLY):
            part = jnp.dot(xt[target(d, 2)], gv[:, d * half + lo:d * half + hi], preferred_element_type=F32)
            for e in range(2):
                early_copy(d, p, e, e).wait_recv()
                part += recvu[d, e, :, lo:hi].astype(F32) * across(upfac[d, e, 0:1], hi - lo)
            sendb[d, 2, :, lo:hi] = part.astype(BF16)
        for p, (lo, hi) in enumerate(rest):
            part = jnp.dot(xt[target(d, 2)], gv[:, d * half + lo:d * half + hi], preferred_element_type=F32)
            ring_copy(d, 0, p).wait_recv()
            sendb[d, 2, :, lo:hi] = (part + recvb[d, 0, :, lo:hi].astype(F32)).astype(BF16)
        ring_copy(d, 2).start()

    @pl.loop(3, steps - 1)
    def _(i):
        step(i)

    step(steps - 1)

    for d in range(2):
        for s in range(PIECES):
            part = term(z, d, s)
            if s == 0:
                ring_copy(1 - d, steps - 2).wait_recv()
            fin[d * PIECES + s] = part + recvb[1 - d, steps - 2, :, cols(s)].astype(F32)

    len_swap.wait_send()
    for d in range(2):
        up_copy(d).wait_send()
        for e in range(2):
            for p in range(len(EARLY)):
                early_copy(d, p, e, e).wait_send()
            g_swap(d, e).wait_send()
        ring_copy(d, 0, 1).wait_send()
        for i in range(steps - 1):
            ring_copy(d, i).wait_send()
    for j in range(side):
        col_copy(1, j, sec_y).wait_send()
        if j:
            row_copy(j, sec_x).wait_send()
            col_copy(0, j, sec_y).wait_send()

    @pl.loop(0, n_chips)
    def _(k):
        xb_swap(k).wait_send()

    for s in range(PIECES):
        for d in range(2):
            c = d * PIECES + s
            if s == 0 or s == PIECES - 1:
                ring_copy(d, steps - 1, int(s > 0)).wait_recv()
            done = (fin[c] + recvb[d, steps - 1, :, cols(s)].astype(F32)) * weight
            out_ref[:, cols(c)] = done.astype(out_ref.dtype)

    for d in range(2):
        for part in range(2):
            ring_copy(d, steps - 1, part).wait_send()


def shards(layer_inputs, output_grads, lengths):
    n_dp, n_sec = lax.axis_size("dp"), lax.axis_size("section")
    inputs = layer_inputs[0, 0]
    grads = output_grads[0, 0]
    seq, din = inputs.shape
    dout = grads.shape[1]
    rows = din // n_dp
    n_chips = n_dp // 2
    steps = n_chips - 1
    half = dout // 2
    width = half // PIECES
    side = math.isqrt(n_sec)
    gone = EARLY[-1][1]
    weight = math.sqrt(din * dout * n_sec / n_dp)
    dma = pltpu.SemaphoreType.DMA
    vmem = pltpu.VMEM
    out = pl.pallas_call(
        functools.partial(kernel, (n_chips, side, rows), weight),
        out_shape=jax.ShapeDtypeStruct((rows, dout), BF16),
        in_specs=[
            pl.BlockSpec(memory_space=pltpu.SMEM),
            pl.BlockSpec(memory_space=pl.ANY),
            pl.BlockSpec(memory_space=pl.ANY),
        ],
        out_specs=pl.BlockSpec(memory_space=pltpu.VMEM),
        scratch_shapes=dict(
            xe=vmem((seq, 2 * rows), BF16),
            xv=vmem((seq, din), BF16),
            xb=vmem((n_chips, seq, rows), BF16),
            gv=vmem((2 * seq, dout), BF16),
            xt=vmem((n_chips, rows, 2 * seq), BF16),
            sendb=vmem((2, steps, rows, half), BF16),
            recvb=vmem((2, steps, rows, half), BF16),
            sendu=vmem((2, 2, rows, gone), BF16),
            recvu=vmem((2, 2, rows, gone), BF16),
            pre=vmem((2, 2, rows, half - width - gone), F32),
            fin=vmem((2 * PIECES, rows, width), F32),
            gin=vmem((seq, seq), F32),
            gout=vmem((seq, seq), F32),
            row_tile=vmem((8, 128), F32),
            col_tile=vmem((8, 128), F32),
            rows_in=vmem((side, 8, 128), F32),
            cols_in=vmem((2, side, 8, 128), F32),
            lens=vmem((2, 8, 128), F32),
            facs=vmem((2, 8, 128), F32),
            upfac=vmem((2, 2, 8, 128), F32),
            xe_sem=dma,
            xv_sem=dma,
            g_sem=dma((2, 2)),
            xb_send=dma((n_chips,)),
            xb_recv=dma((n_chips,)),
            g_send=dma((2, 2)),
            g_recv=dma((2, 2)),
            len_sem=dma((2,)),
            row_send=dma((side,)),
            row_recv=dma((side,)),
            col_send=dma((2, side)),
            col_recv=dma((2, side)),
            early_send=dma((2, len(EARLY), 2)),
            early_recv=dma((2, len(EARLY), 2)),
            up_send=dma((2,)),
            up_recv=dma((2,)),
            ring_send=dma((2, steps + 2)),
            ring_recv=dma((2, steps + 2)),
        ),
        compiler_params=pltpu.CompilerParams(
            collective_id=0, has_side_effects=True, vmem_limit_bytes=52 * 2**20
        ),
        cost_estimate=pl.CostEstimate(
            flops=2 * seq * din * dout + 2 * seq * seq * (din + dout), bytes_accessed=2 * seq * (din + dout),
            transcendentals=0,
        ),
    )(lengths, inputs, grads)
    return out[None]


def solution(mesh):
    placed = (P("section", "dp", None, None), P("section", "dp", None, None), P("dp"))
    return jax.shard_map(
        shards, mesh=mesh, in_specs=placed, out_specs=P("section", "dp", None), check_vma=False
    )
```

```python
import functools
import math

import jax
import jax.numpy as jnp
from jax import lax
from jax.experimental import pallas as pl
from jax.experimental.pallas import tpu as pltpu
from jax.sharding import PartitionSpec as P

F32 = jnp.float32
BF16 = jnp.bfloat16
MESH = pl.DeviceIdType.MESH
PIECES = 3
EARLY = ((0, 512), (512, 1152))


def kernel(dims, weight, len_ref, x_ref, g_ref, out_ref, xe, xv, xb, gv, xt, sendb, recvb, sendu, recvu, pre, fin, gin, gout,
           row_tile, col_tile, rows_in, cols_in, lens, facs, upfac, xe_sem, xv_sem, g_sem, xb_send, xb_recv, g_send, g_recv,
           len_sem, row_send, row_recv, col_send, col_recv, early_send, early_recv, up_send, up_recv, ring_send, ring_recv):
    n_chips, side, rows = dims
    seq = x_ref.shape[0]
    half = sendb.shape[3]
    width = half // PIECES
    gone = EARLY[-1][1]
    rest = ((gone, half - width), (half - width, half))
    mid = seq // 2
    steps = n_chips - 1
    dp = lax.axis_index("dp")
    sec = lax.axis_index("section")
    z = lax.div(dp, 2)
    core = lax.rem(dp, 2)
    partner = dp + 1 - 2 * core
    ahead = lax.rem(dp + 2, 2 * n_chips)
    behind = lax.rem(dp + 2 * n_chips - 2, 2 * n_chips)
    ring_to = (ahead, behind)
    sec_x = lax.div(sec, side)
    sec_y = lax.rem(sec, side)

    def in_row(j):
        return lax.rem(sec_x + j, side) * side + sec_y

    def in_col(j):
        return sec_x * side + lax.rem(sec_y + j, side)

    def owner(k):
        far = lax.div(k + 1, 2)
        turn = jnp.where(lax.rem(k, 2) == 1, n_chips - far, far)
        return lax.rem(z + n_chips // 2 + turn, n_chips)

    def x_cols(k, c):
        return pl.ds(pl.multiple_of((2 * k + c) * rows, 128), rows)

    def g_cols(h, part, cut):
        return pl.ds(h * half + cut, half - cut) if part else pl.ds(h * half, cut)

    def g_copy(h, part):
        cols = g_cols(h, part, EARLY[0][1])
        return pltpu.make_async_copy(g_ref.at[:, cols], gv.at[pl.ds(0, seq), cols], g_sem.at[h, part])

    def g_swap(h, part):
        cols = g_cols(h, part, gone)
        return pltpu.make_async_remote_copy(
            g_ref.at[:, cols], gv.at[pl.ds(seq, seq), cols], g_send.at[h, part], g_recv.at[h, part],
            device_id=(partner, sec), device_id_type=MESH)

    def xb_swap(k):
        return pltpu.make_async_remote_copy(
            x_ref.at[:, x_cols(k, 1 - core)], xb.at[k], xb_send.at[k], xb_recv.at[k],
            device_id=(partner, sec), device_id_type=MESH)

    first = owner(0)
    xe_cols = pl.ds(pl.multiple_of(2 * first * rows, 128), 2 * rows)
    xe_copy = pltpu.make_async_copy(x_ref.at[:, xe_cols], xe, xe_sem)
    x_copy = pltpu.make_async_copy(x_ref, xv, xv_sem)
    xe_copy.start()
    for h in range(2):
        g_copy(h, 0).start()

    barrier = pltpu.get_barrier_semaphore()
    peers = [(peer + other, sec) for peer in ring_to for other in (0, partner - dp)]
    peers += [(dp, in_row(j)) for j in range(1, side)] + [(dp, in_col(j)) for j in range(1, side)]
    peers += [(partner, in_col(j)) for j in range(side)]
    for peer in peers:
        pl.semaphore_signal(barrier, inc=1, device_id=peer, device_id_type=MESH)
    x_copy.start()
    for h in range(2):
        g_copy(h, 1).start()

    xe_copy.wait()
    token = lax.broadcasted_iota(jnp.int32, xe.shape, 0)
    xet = jnp.where(token < len_ref[0], xe[...].astype(F32), 0.0).T.astype(BF16)

    def early_copy(d, p, e, slot):
        block = pl.ds(EARLY[p][0], EARLY[p][1] - EARLY[p][0])
        return pltpu.make_async_remote_copy(
            sendu.at[d, e, :, block], recvu.at[d, slot, :, block], early_send.at[d, p, e], early_recv.at[d, p, slot],
            device_id=(ring_to[d] - core + e, sec), device_id_type=MESH)

    def early_terms(p):
        for d in range(2):
            if p < 2:
                g_copy(d, p).wait()
            lo, hi = EARLY[p]
            early = jnp.dot(xet, gv[:seq, d * half + lo:d * half + hi], preferred_element_type=F32).astype(BF16)
            for e in range(2):
                sendu[d, e, :, lo:hi] = early[e * rows:(e + 1) * rows]

    def early_start(p):
        for e in range(2):
            for d in range(2):
                early_copy(d, p, e, lax.rem(core + e, 2)).start()

    early_terms(0)
    lens[0] = jnp.full(lens.shape[1:], len_ref[0], F32)
    pl.semaphore_wait(barrier, len(peers))
    early_start(0)
    len_swap = pltpu.make_async_remote_copy(
        lens.at[0], lens.at[1], len_sem.at[0], len_sem.at[1], device_id=(partner, sec), device_id_type=MESH)
    len_swap.start()
    xb_swap(first).start()
    for h in range(2):
        g_swap(h, 1).start()

    def gram(acc, block, new=False):
        nt = (((1,), (1,)), ((), ()))
        left = lax.dot_general(block[:mid], block[:mid], nt, preferred_element_type=F32)
        right = lax.dot_general(block, block[mid:], nt, preferred_element_type=F32)
        if new:
            acc[:mid, :mid] = left
            acc[:, mid:] = right
        else:
            acc[:mid, :mid] += left
            acc[:, mid:] += right

    x_copy.wait()
    gram(gin, xv[...], True)
    for p in range(1, len(EARLY)):
        early_terms(p)
        early_start(p)
    for h in range(2):
        gram(gout, gv[:seq, h * half:(h + 1) * half], h == 0)

    row = lax.broadcasted_iota(jnp.int32, (seq, mid), 0)
    col = lax.broadcasted_iota(jnp.int32, (seq, mid), 1)
    n_live = len_ref[0]
    left_live = (row[:mid] < n_live) & (col[:mid] < n_live)
    left = jnp.where(left_live, gin[:mid, :mid] * gout[:mid, :mid], 0.0)
    twice = jnp.where(row < mid, 2.0, 1.0)
    right_live = (row < n_live) & (col + mid < n_live)
    right = jnp.where(right_live, gin[:, mid:] * gout[:, mid:] * twice, 0.0)
    cells = left + right[:mid] + right[mid:]
    norm = jnp.sum(jnp.sum(cells, axis=0, keepdims=True), axis=1, keepdims=True)
    row_tile[...] = jnp.broadcast_to(norm, row_tile.shape)

    def row_copy(j, frm):
        return pltpu.make_async_remote_copy(
            row_tile, rows_in.at[frm], row_send.at[j], row_recv.at[frm], device_id=(dp, in_row(j)), device_id_type=MESH)

    def col_copy(e, j, frm):
        return pltpu.make_async_remote_copy(
            col_tile, cols_in.at[e, frm], col_send.at[e, j], col_recv.at[e, frm],
            device_id=(partner if e else dp, in_col(j)), device_id_type=MESH)

    for j in range(1, side):
        row_copy(j, sec_x).start()
    rows_in[sec_x] = row_tile[...]

    token = lax.broadcasted_iota(jnp.int32, (seq, rows), 0).astype(F32)

    def turn(k):
        xb_swap(k).wait_recv()
        for e, block in enumerate((xv[:, x_cols(k, core)], xb[k])):
            block = jnp.where(token < lens[e, 0:1, :], block.astype(F32), 0.0)
            xt[k, :, e * seq:(e + 1) * seq] = block.T.astype(BF16)

    def scale(k):
        for e in range(2):
            factor = facs[e, 0:1, :]
            for j in range(seq // 128):
                cols = slice(e * seq + j * 128, e * seq + (j + 1) * 128)
                xt[k, :, cols] = (xt[k, :, cols].astype(F32) * factor).astype(BF16)

    for j in range(1, side):
        row_copy(j, lax.rem(sec_x + j, side)).wait_recv()
    col_tile[...] = jnp.sum(rows_in[...], axis=0)
    for j in range(side):
        col_copy(1, j, sec_y).start()
        if j:
            col_copy(0, j, sec_y).start()
    cols_in[0, sec_y] = col_tile[...]
    for k in (1, 2):
        xb_swap(owner(k)).start()
    for h in range(2):
        g_swap(h, 0).start()

    len_swap.wait_recv()
    turn(first)
    lo, hi = rest[0]
    for d in range(2):
        g_swap(d, 1).wait_recv()
        for e in range(2):
            tokens = slice(e * seq, (e + 1) * seq)
            pre[d, e] = jnp.dot(
                xt[first, :, tokens], gv[tokens, d * half + lo:d * half + hi], preferred_element_type=F32)

    for j in range(side):
        frm = lax.rem(sec_y + j, side)
        col_copy(1, j, frm).wait_recv()
        if j:
            col_copy(0, j, frm).wait_recv()
    for e in range(2):
        facs[e] = jnp.minimum(1.0, 1.0 / jnp.sqrt(jnp.sum(cols_in[e], axis=0) + 1e-06))

    def up_copy(d):
        return pltpu.make_async_remote_copy(
            facs, upfac.at[d], up_send.at[d], up_recv.at[d], device_id=(ring_to[d], sec), device_id_type=MESH)

    def ring_copy(d, i, part=0):
        block = pl.ds(0, half)
        sem = i + part
        if isinstance(i, int) and i == 0:
            block = pl.ds(rest[part][0], rest[part][1] - rest[part][0])
            sem = part * (steps + 1)
        elif isinstance(i, int) and i == steps - 1:
            block = pl.ds(half - width, width) if part else pl.ds(0, half - width)
        return pltpu.make_async_remote_copy(
            sendb.at[d, i, :, block], recvb.at[d, i, :, block], ring_send.at[d, sem], ring_recv.at[d, sem],
            device_id=(ring_to[d], sec), device_id_type=MESH)

    def term(k, h, s):
        return jnp.dot(xt[k], gv[:, pl.ds(pl.multiple_of(h * half + s * width, 128), width)], preferred_element_type=F32)

    def target(d, i):
        dist = n_chips // 2 - lax.div(i + 1, 2)
        return lax.rem(z + dist, n_chips) if d == 0 else lax.rem(z + n_chips - dist, n_chips)

    def cols(s):
        return slice(s * width, (s + 1) * width)

    def across(factor, n):
        return jnp.concatenate([factor] * (n // 128), axis=1)

    def step(i, add=True):
        for d in range(2):
            for s in range(PIECES):
                part = term(target(d, i), lax.rem(i + d, 2), s)
                if add:
                    if s == 0:
                        ring_copy(d, i - 2).wait_recv()
                    part += recvb[d, i - 2, :, cols(s)].astype(F32)
                sendb[d, i, :, cols(s)] = part.astype(BF16)
                if isinstance(i, int) and i == steps - 1 and s == PIECES - 2:
                    ring_copy(d, i).start()
            ring_copy(d, i, isinstance(i, int) and i == steps - 1).start()

    lo, hi = rest[0]
    for d in range(2):
        own, other = (pre[d, e] * across(facs[e, 0:1], hi - lo) for e in range(2))
        sendb[d, 0, :, lo:hi] = (own + other).astype(BF16)
        ring_copy(d, 0).start()
    scale(first)
    lo, hi = rest[1]
    for d in range(2):
        part = jnp.dot(xt[first], gv[:, d * half + lo:d * half + hi], preferred_element_type=F32)
        sendb[d, 0, :, lo:hi] = part.astype(BF16)
        ring_copy(d, 0, 1).start()
    for d in range(2):
        up_copy(d).start()

    @pl.loop(3, n_chips)
    def _(k):
        xb_swap(owner(k)).start()

    @pl.loop(1, 3)
    def _(k):
        turn(owner(k))
        scale(owner(k))

    for h in range(2):
        g_swap(h, 0).wait_recv()
    step(1, add=False)

    @pl.loop(3, n_chips)
    def _(k):
        turn(owner(k))
        scale(owner(k))

    for d in range(2):
        up_copy(d).wait_recv()
        for p, (lo, hi) in enumerate(EARLY):
            part = jnp.dot(xt[target(d, 2)], gv[:, d * half + lo:d * half + hi], preferred_element_type=F32)
            for e in range(2):
                early_copy(d, p, e, e).wait_recv()
                part += recvu[d, e, :, lo:hi].astype(F32) * across(upfac[d, e, 0:1], hi - lo)
            sendb[d, 2, :, lo:hi] = part.astype(BF16)
        for p, (lo, hi) in enumerate(rest):
            part = jnp.dot(xt[target(d, 2)], gv[:, d * half + lo:d * half + hi], preferred_element_type=F32)
            ring_copy(d, 0, p).wait_recv()
            sendb[d, 2, :, lo:hi] = (part + recvb[d, 0, :, lo:hi].astype(F32)).astype(BF16)
        ring_copy(d, 2).start()

    @pl.loop(3, steps - 1)
    def _(i):
        step(i)

    step(steps - 1)

    for d in range(2):
        for s in range(PIECES):
            part = term(z, d, s)
            if s == 0:
                ring_copy(1 - d, steps - 2).wait_recv()
            fin[d * PIECES + s] = part + recvb[1 - d, steps - 2, :, cols(s)].astype(F32)

    len_swap.wait_send()
    for d in range(2):
        up_copy(d).wait_send()
        for e in range(2):
            for p in range(len(EARLY)):
                early_copy(d, p, e, e).wait_send()
            g_swap(d, e).wait_send()
        ring_copy(d, 0, 1).wait_send()
        for i in range(steps - 1):
            ring_copy(d, i).wait_send()
    for j in range(side):
        col_copy(1, j, sec_y).wait_send()
        if j:
            row_copy(j, sec_x).wait_send()
            col_copy(0, j, sec_y).wait_send()

    @pl.loop(0, n_chips)
    def _(k):
        xb_swap(k).wait_send()

    for s in range(PIECES):
        for d in range(2):
            c = d * PIECES + s
            if s == 0 or s == PIECES - 1:
                ring_copy(d, steps - 1, int(s > 0)).wait_recv()
            done = (fin[c] + recvb[d, steps - 1, :, cols(s)].astype(F32)) * weight
            out_ref[:, cols(c)] = done.astype(out_ref.dtype)

    for d in range(2):
        for part in range(2):
            ring_copy(d, steps - 1, part).wait_send()


def shards(layer_inputs, output_grads, lengths):
    n_dp, n_sec = lax.axis_size("dp"), lax.axis_size("section")
    inputs = layer_inputs[0, 0]
    grads = output_grads[0, 0]
    seq, din = inputs.shape
    dout = grads.shape[1]
    rows = din // n_dp
    n_chips = n_dp // 2
    steps = n_chips - 1
    half = dout // 2
    width = half // PIECES
    side = math.isqrt(n_sec)
    gone = EARLY[-1][1]
    weight = math.sqrt(din * dout * n_sec / n_dp)
    dma = pltpu.SemaphoreType.DMA
    vmem = pltpu.VMEM
    out = pl.pallas_call(
        functools.partial(kernel, (n_chips, side, rows), weight),
        out_shape=jax.ShapeDtypeStruct((rows, dout), BF16),
        in_specs=[
            pl.BlockSpec(memory_space=pltpu.SMEM),
            pl.BlockSpec(memory_space=pl.ANY),
            pl.BlockSpec(memory_space=pl.ANY),
        ],
        out_specs=pl.BlockSpec(memory_space=pltpu.VMEM),
        scratch_shapes=dict(
            xe=vmem((seq, 2 * rows), BF16),
            xv=vmem((seq, din), BF16),
            xb=vmem((n_chips, seq, rows), BF16),
            gv=vmem((2 * seq, dout), BF16),
            xt=vmem((n_chips, rows, 2 * seq), BF16),
            sendb=vmem((2, steps, rows, half), BF16),
            recvb=vmem((2, steps, rows, half), BF16),
            sendu=vmem((2, 2, rows, gone), BF16),
            recvu=vmem((2, 2, rows, gone), BF16),
            pre=vmem((2, 2, rows, half - width - gone), F32),
            fin=vmem((2 * PIECES, rows, width), F32),
            gin=vmem((seq, seq), F32),
            gout=vmem((seq, seq), F32),
            row_tile=vmem((8, 128), F32),
            col_tile=vmem((8, 128), F32),
            rows_in=vmem((side, 8, 128), F32),
            cols_in=vmem((2, side, 8, 128), F32),
            lens=vmem((2, 8, 128), F32),
            facs=vmem((2, 8, 128), F32),
            upfac=vmem((2, 2, 8, 128), F32),
            xe_sem=dma,
            xv_sem=dma,
            g_sem=dma((2, 2)),
            xb_send=dma((n_chips,)),
            xb_recv=dma((n_chips,)),
            g_send=dma((2, 2)),
            g_recv=dma((2, 2)),
            len_sem=dma((2,)),
            row_send=dma((side,)),
            row_recv=dma((side,)),
            col_send=dma((2, side)),
            col_recv=dma((2, side)),
            early_send=dma((2, len(EARLY), 2)),
            early_recv=dma((2, len(EARLY), 2)),
            up_send=dma((2,)),
            up_recv=dma((2,)),
            ring_send=dma((2, steps + 2)),
            ring_recv=dma((2, steps + 2)),
        ),
        compiler_params=pltpu.CompilerParams(
            collective_id=0, has_side_effects=True, vmem_limit_bytes=52 * 2**20
        ),
        cost_estimate=pl.CostEstimate(
            flops=2 * seq * din * dout + 2 * seq * seq * (din + dout), bytes_accessed=2 * seq * (din + dout),
            transcendentals=0,
        ),
    )(lengths, inputs, grads)
    return out[None]


def solution(mesh):
    placed = (P("section", "dp", None, None), P("section", "dp", None, None), P("dp"))
    return jax.shard_map(
        shards, mesh=mesh, in_specs=placed, out_specs=P("section", "dp", None), check_vma=False
    )
```

```python
import functools
import math

import jax
import jax.numpy as jnp
from jax import lax
from jax.experimental import pallas as pl
from jax.experimental.pallas import tpu as pltpu
from jax.sharding import PartitionSpec as P

F32 = jnp.float32
BF16 = jnp.bfloat16
MESH = pl.DeviceIdType.MESH
PIECES = 3
EARLY = ((0, 768), (768, 1152))


def kernel(dims, weight, len_ref, x_ref, g_ref, out_ref, xe, xv, xb, gv, xt, sendb, recvb, sendu, recvu, pre, fin, gin, gout,
           row_tile, col_tile, rows_in, cols_in, lens, facs, upfac, xe_sem, xv_sem, g_sem, xb_send, xb_recv, g_send, g_recv,
           len_sem, row_send, row_recv, col_send, col_recv, early_send, early_recv, up_send, up_recv, ring_send, ring_recv):
    n_chips, side, rows = dims
    seq = x_ref.shape[0]
    half = sendb.shape[3]
    width = half // PIECES
    gone = EARLY[-1][1]
    rest = ((gone, half - width), (half - width, half))
    mid = seq // 2
    steps = n_chips - 1
    dp = lax.axis_index("dp")
    sec = lax.axis_index("section")
    z = lax.div(dp, 2)
    core = lax.rem(dp, 2)
    partner = dp + 1 - 2 * core
    ahead = lax.rem(dp + 2, 2 * n_chips)
    behind = lax.rem(dp + 2 * n_chips - 2, 2 * n_chips)
    ring_to = (ahead, behind)
    sec_x = lax.div(sec, side)
    sec_y = lax.rem(sec, side)

    def in_row(j):
        return lax.rem(sec_x + j, side) * side + sec_y

    def in_col(j):
        return sec_x * side + lax.rem(sec_y + j, side)

    def owner(k):
        far = lax.div(k + 1, 2)
        turn = jnp.where(lax.rem(k, 2) == 1, n_chips - far, far)
        return lax.rem(z + n_chips // 2 + turn, n_chips)

    def x_cols(k, c):
        return pl.ds(pl.multiple_of((2 * k + c) * rows, 128), rows)

    def g_cols(h, part):
        return pl.ds(h * half + gone, half - gone) if part else pl.ds(h * half, gone)

    def g_copy(h, part):
        cols = g_cols(h, part)
        return pltpu.make_async_copy(g_ref.at[:, cols], gv.at[pl.ds(0, seq), cols], g_sem.at[h, part])

    def g_swap(h, part):
        cols = g_cols(h, part)
        return pltpu.make_async_remote_copy(
            g_ref.at[:, cols], gv.at[pl.ds(seq, seq), cols], g_send.at[h, part], g_recv.at[h, part],
            device_id=(partner, sec), device_id_type=MESH)

    def xb_swap(k):
        return pltpu.make_async_remote_copy(
            x_ref.at[:, x_cols(k, 1 - core)], xb.at[k], xb_send.at[k], xb_recv.at[k],
            device_id=(partner, sec), device_id_type=MESH)

    first = owner(0)
    xe_cols = pl.ds(pl.multiple_of(2 * first * rows, 128), 2 * rows)
    xe_copy = pltpu.make_async_copy(x_ref.at[:, xe_cols], xe, xe_sem)
    x_copy = pltpu.make_async_copy(x_ref, xv, xv_sem)
    xe_copy.start()
    for h in range(2):
        g_copy(h, 0).start()

    barrier = pltpu.get_barrier_semaphore()
    peers = [(peer + other, sec) for peer in ring_to for other in (0, partner - dp)]
    peers += [(dp, in_row(j)) for j in range(1, side)] + [(dp, in_col(j)) for j in range(1, side)]
    peers += [(partner, in_col(j)) for j in range(side)]
    for peer in peers:
        pl.semaphore_signal(barrier, inc=1, device_id=peer, device_id_type=MESH)
    x_copy.start()
    for h in range(2):
        g_copy(h, 1).start()

    xe_copy.wait()
    token = lax.broadcasted_iota(jnp.int32, xe.shape, 0)
    xet = jnp.where(token < len_ref[0], xe[...].astype(F32), 0.0).T.astype(BF16)

    def early_copy(d, p, e, slot):
        block = pl.ds(EARLY[p][0], EARLY[p][1] - EARLY[p][0])
        return pltpu.make_async_remote_copy(
            sendu.at[d, e, :, block], recvu.at[d, slot, :, block], early_send.at[d, p, e], early_recv.at[d, p, slot],
            device_id=(ring_to[d] - core + e, sec), device_id_type=MESH)

    def early_terms(p):
        for d in range(2):
            if p == 0:
                g_copy(d, 0).wait()
            lo, hi = EARLY[p]
            early = jnp.dot(xet, gv[:seq, d * half + lo:d * half + hi], preferred_element_type=F32).astype(BF16)
            for e in range(2):
                sendu[d, e, :, lo:hi] = early[e * rows:(e + 1) * rows]

    def early_start(p):
        for e in range(2):
            for d in range(2):
                early_copy(d, p, e, lax.rem(core + e, 2)).start()

    early_terms(0)
    lens[0] = jnp.full(lens.shape[1:], len_ref[0], F32)
    pl.semaphore_wait(barrier, len(peers))
    early_start(0)
    len_swap = pltpu.make_async_remote_copy(
        lens.at[0], lens.at[1], len_sem.at[0], len_sem.at[1], device_id=(partner, sec), device_id_type=MESH)
    len_swap.start()
    xb_swap(first).start()
    for h in range(2):
        g_swap(h, 1).start()

    def gram(acc, block, new=False):
        nt = (((1,), (1,)), ((), ()))
        left = lax.dot_general(block[:mid], block[:mid], nt, preferred_element_type=F32)
        right = lax.dot_general(block, block[mid:], nt, preferred_element_type=F32)
        if new:
            acc[:mid, :mid] = left
            acc[:, mid:] = right
        else:
            acc[:mid, :mid] += left
            acc[:, mid:] += right

    x_copy.wait()
    gram(gin, xv[...], True)
    for p in range(1, len(EARLY)):
        early_terms(p)
        early_start(p)
    for h in range(2):
        g_copy(h, 1).wait()
        gram(gout, gv[:seq, h * half:(h + 1) * half], h == 0)

    row = lax.broadcasted_iota(jnp.int32, (seq, mid), 0)
    col = lax.broadcasted_iota(jnp.int32, (seq, mid), 1)
    n_live = len_ref[0]
    left_live = (row[:mid] < n_live) & (col[:mid] < n_live)
    left = jnp.where(left_live, gin[:mid, :mid] * gout[:mid, :mid], 0.0)
    twice = jnp.where(row < mid, 2.0, 1.0)
    right_live = (row < n_live) & (col + mid < n_live)
    right = jnp.where(right_live, gin[:, mid:] * gout[:, mid:] * twice, 0.0)
    cells = left + right[:mid] + right[mid:]
    norm = jnp.sum(jnp.sum(cells, axis=0, keepdims=True), axis=1, keepdims=True)
    row_tile[...] = jnp.broadcast_to(norm, row_tile.shape)

    def row_copy(j, frm):
        return pltpu.make_async_remote_copy(
            row_tile, rows_in.at[frm], row_send.at[j], row_recv.at[frm], device_id=(dp, in_row(j)), device_id_type=MESH)

    def col_copy(e, j, frm):
        return pltpu.make_async_remote_copy(
            col_tile, cols_in.at[e, frm], col_send.at[e, j], col_recv.at[e, frm],
            device_id=(partner if e else dp, in_col(j)), device_id_type=MESH)

    for j in range(1, side):
        row_copy(j, sec_x).start()
    rows_in[sec_x] = row_tile[...]

    token = lax.broadcasted_iota(jnp.int32, (seq, rows), 0).astype(F32)

    def turn(k):
        xb_swap(k).wait_recv()
        for e, block in enumerate((xv[:, x_cols(k, core)], xb[k])):
            block = jnp.where(token < lens[e, 0:1, :], block.astype(F32), 0.0)
            xt[k, :, e * seq:(e + 1) * seq] = block.T.astype(BF16)

    def scale(k):
        for e in range(2):
            factor = facs[e, 0:1, :]
            for j in range(seq // 128):
                cols = slice(e * seq + j * 128, e * seq + (j + 1) * 128)
                xt[k, :, cols] = (xt[k, :, cols].astype(F32) * factor).astype(BF16)

    for j in range(1, side):
        row_copy(j, lax.rem(sec_x + j, side)).wait_recv()
    col_tile[...] = jnp.sum(rows_in[...], axis=0)
    for j in range(side):
        col_copy(1, j, sec_y).start()
        if j:
            col_copy(0, j, sec_y).start()
    cols_in[0, sec_y] = col_tile[...]
    for k in (1, 2):
        xb_swap(owner(k)).start()
    for h in range(2):
        g_swap(h, 0).start()

    len_swap.wait_recv()
    turn(first)
    lo, hi = rest[0]
    for d in range(2):
        g_swap(d, 1).wait_recv()
        for e in range(2):
            tokens = slice(e * seq, (e + 1) * seq)
            pre[d, e] = jnp.dot(
                xt[first, :, tokens], gv[tokens, d * half + lo:d * half + hi], preferred_element_type=F32)

    for j in range(side):
        frm = lax.rem(sec_y + j, side)
        col_copy(1, j, frm).wait_recv()
        if j:
            col_copy(0, j, frm).wait_recv()
    for e in range(2):
        facs[e] = jnp.minimum(1.0, 1.0 / jnp.sqrt(jnp.sum(cols_in[e], axis=0) + 1e-06))

    def up_copy(d):
        return pltpu.make_async_remote_copy(
            facs, upfac.at[d], up_send.at[d], up_recv.at[d], device_id=(ring_to[d], sec), device_id_type=MESH)

    def ring_copy(d, i, part=0):
        block = pl.ds(0, half)
        sem = i + part
        if isinstance(i, int) and i == 0:
            block = pl.ds(rest[part][0], rest[part][1] - rest[part][0])
            sem = part * (steps + 1)
        elif isinstance(i, int) and i == steps - 1:
            block = pl.ds(half - width, width) if part else pl.ds(0, half - width)
        return pltpu.make_async_remote_copy(
            sendb.at[d, i, :, block], recvb.at[d, i, :, block], ring_send.at[d, sem], ring_recv.at[d, sem],
            device_id=(ring_to[d], sec), device_id_type=MESH)

    def term(k, h, s):
        return jnp.dot(xt[k], gv[:, pl.ds(pl.multiple_of(h * half + s * width, 128), width)], preferred_element_type=F32)

    def target(d, i):
        dist = n_chips // 2 - lax.div(i + 1, 2)
        return lax.rem(z + dist, n_chips) if d == 0 else lax.rem(z + n_chips - dist, n_chips)

    def cols(s):
        return slice(s * width, (s + 1) * width)

    def across(factor, n):
        return jnp.concatenate([factor] * (n // 128), axis=1)

    def step(i, add=True):
        for d in range(2):
            for s in range(PIECES):
                part = term(target(d, i), lax.rem(i + d, 2), s)
                if add:
                    if s == 0:
                        ring_copy(d, i - 2).wait_recv()
                    part += recvb[d, i - 2, :, cols(s)].astype(F32)
                sendb[d, i, :, cols(s)] = part.astype(BF16)
                if isinstance(i, int) and i == steps - 1 and s == PIECES - 2:
                    ring_copy(d, i).start()
            ring_copy(d, i, isinstance(i, int) and i == steps - 1).start()

    lo, hi = rest[0]
    for d in range(2):
        own, other = (pre[d, e] * across(facs[e, 0:1], hi - lo) for e in range(2))
        sendb[d, 0, :, lo:hi] = (own + other).astype(BF16)
        ring_copy(d, 0).start()
    scale(first)
    lo, hi = rest[1]
    for d in range(2):
        part = jnp.dot(xt[first], gv[:, d * half + lo:d * half + hi], preferred_element_type=F32)
        sendb[d, 0, :, lo:hi] = part.astype(BF16)
        ring_copy(d, 0, 1).start()
    for d in range(2):
        up_copy(d).start()

    @pl.loop(3, n_chips)
    def _(k):
        xb_swap(owner(k)).start()

    @pl.loop(1, 3)
    def _(k):
        turn(owner(k))
        scale(owner(k))

    for h in range(2):
        g_swap(h, 0).wait_recv()
    step(1, add=False)

    @pl.loop(3, n_chips)
    def _(k):
        turn(owner(k))
        scale(owner(k))

    for d in range(2):
        up_copy(d).wait_recv()
        for p, (lo, hi) in enumerate(EARLY):
            part = jnp.dot(xt[target(d, 2)], gv[:, d * half + lo:d * half + hi], preferred_element_type=F32)
            for e in range(2):
                early_copy(d, p, e, e).wait_recv()
                part += recvu[d, e, :, lo:hi].astype(F32) * across(upfac[d, e, 0:1], hi - lo)
            sendb[d, 2, :, lo:hi] = part.astype(BF16)
        for p, (lo, hi) in enumerate(rest):
            part = jnp.dot(xt[target(d, 2)], gv[:, d * half + lo:d * half + hi], preferred_element_type=F32)
            ring_copy(d, 0, p).wait_recv()
            sendb[d, 2, :, lo:hi] = (part + recvb[d, 0, :, lo:hi].astype(F32)).astype(BF16)
        ring_copy(d, 2).start()

    @pl.loop(3, steps - 1)
    def _(i):
        step(i)

    step(steps - 1)

    for d in range(2):
        for s in range(PIECES):
            part = term(z, d, s)
            if s == 0:
                ring_copy(1 - d, steps - 2).wait_recv()
            fin[d * PIECES + s] = part + recvb[1 - d, steps - 2, :, cols(s)].astype(F32)

    len_swap.wait_send()
    for d in range(2):
        up_copy(d).wait_send()
        for e in range(2):
            for p in range(len(EARLY)):
                early_copy(d, p, e, e).wait_send()
            g_swap(d, e).wait_send()
        ring_copy(d, 0, 1).wait_send()
        for i in range(steps - 1):
            ring_copy(d, i).wait_send()
    for j in range(side):
        col_copy(1, j, sec_y).wait_send()
        if j:
            row_copy(j, sec_x).wait_send()
            col_copy(0, j, sec_y).wait_send()

    @pl.loop(0, n_chips)
    def _(k):
        xb_swap(k).wait_send()

    for s in range(PIECES):
        for d in range(2):
            c = d * PIECES + s
            if s == 0 or s == PIECES - 1:
                ring_copy(d, steps - 1, int(s > 0)).wait_recv()
            done = (fin[c] + recvb[d, steps - 1, :, cols(s)].astype(F32)) * weight
            out_ref[:, cols(c)] = done.astype(out_ref.dtype)

    for d in range(2):
        for part in range(2):
            ring_copy(d, steps - 1, part).wait_send()


def shards(layer_inputs, output_grads, lengths):
    n_dp, n_sec = lax.axis_size("dp"), lax.axis_size("section")
    inputs = layer_inputs[0, 0]
    grads = output_grads[0, 0]
    seq, din = inputs.shape
    dout = grads.shape[1]
    rows = din // n_dp
    n_chips = n_dp // 2
    steps = n_chips - 1
    half = dout // 2
    width = half // PIECES
    side = math.isqrt(n_sec)
    gone = EARLY[-1][1]
    weight = math.sqrt(din * dout * n_sec / n_dp)
    dma = pltpu.SemaphoreType.DMA
    vmem = pltpu.VMEM
    out = pl.pallas_call(
        functools.partial(kernel, (n_chips, side, rows), weight),
        out_shape=jax.ShapeDtypeStruct((rows, dout), BF16),
        in_specs=[
            pl.BlockSpec(memory_space=pltpu.SMEM),
            pl.BlockSpec(memory_space=pl.ANY),
            pl.BlockSpec(memory_space=pl.ANY),
        ],
        out_specs=pl.BlockSpec(memory_space=pltpu.VMEM),
        scratch_shapes=dict(
            xe=vmem((seq, 2 * rows), BF16),
            xv=vmem((seq, din), BF16),
            xb=vmem((n_chips, seq, rows), BF16),
            gv=vmem((2 * seq, dout), BF16),
            xt=vmem((n_chips, rows, 2 * seq), BF16),
            sendb=vmem((2, steps, rows, half), BF16),
            recvb=vmem((2, steps, rows, half), BF16),
            sendu=vmem((2, 2, rows, gone), BF16),
            recvu=vmem((2, 2, rows, gone), BF16),
            pre=vmem((2, 2, rows, half - width - gone), F32),
            fin=vmem((2 * PIECES, rows, width), F32),
            gin=vmem((seq, seq), F32),
            gout=vmem((seq, seq), F32),
            row_tile=vmem((8, 128), F32),
            col_tile=vmem((8, 128), F32),
            rows_in=vmem((side, 8, 128), F32),
            cols_in=vmem((2, side, 8, 128), F32),
            lens=vmem((2, 8, 128), F32),
            facs=vmem((2, 8, 128), F32),
            upfac=vmem((2, 2, 8, 128), F32),
            xe_sem=dma,
            xv_sem=dma,
            g_sem=dma((2, 2)),
            xb_send=dma((n_chips,)),
            xb_recv=dma((n_chips,)),
            g_send=dma((2, 2)),
            g_recv=dma((2, 2)),
            len_sem=dma((2,)),
            row_send=dma((side,)),
            row_recv=dma((side,)),
            col_send=dma((2, side)),
            col_recv=dma((2, side)),
            early_send=dma((2, len(EARLY), 2)),
            early_recv=dma((2, len(EARLY), 2)),
            up_send=dma((2,)),
            up_recv=dma((2,)),
            ring_send=dma((2, steps + 2)),
            ring_recv=dma((2, steps + 2)),
        ),
        compiler_params=pltpu.CompilerParams(
            collective_id=0, has_side_effects=True, vmem_limit_bytes=52 * 2**20
        ),
        cost_estimate=pl.CostEstimate(
            flops=2 * seq * din * dout + 2 * seq * seq * (din + dout), bytes_accessed=2 * seq * (din + dout),
            transcendentals=0,
        ),
    )(lengths, inputs, grads)
    return out[None]


def solution(mesh):
    placed = (P("section", "dp", None, None), P("section", "dp", None, None), P("dp"))
    return jax.shard_map(
        shards, mesh=mesh, in_specs=placed, out_specs=P("section", "dp", None), check_vma=False
    )
```
